512 devices in a mesh: dp: 16 (over y_lo, z), expert: 32 (over x, y_hi, core).
Axes of the slice: x: 4, y: 8 (y_hi: 4, y_lo: 2; y = y_hi * 2 + y_lo), z: 8, core: 2. Of those that a mesh axis runs over, the one named last changes fastest.
Arguments:
- routes: int32 [65536, 6], P(('dp', 'expert')), may hold values from 0 to 159, all different within a row
- route_weights: float32 [65536, 6], P(('dp', 'expert')), may hold values from 0.02 to 0.5
- hidden_grads: bfloat16 [32, 3072, 1536], P('expert', 'dp'), may hold values from -6 to 6
- expert_weight: bfloat16 [32, 5120, 1536], P('expert', 'dp'), may hold values from -0.15625 to 0.15625
- normed: bfloat16 [65536, 5120], P(('dp', 'expert')), may hold values from -24 to 24
- key_grad: bfloat16 [65536, 64], P(('dp', 'expert')), may hold values from -6 to 6
- rope_weight: bfloat16 [64, 5120], replicated, may hold values from -0.75 to 0.75
Outputs:
- token_grad: bfloat16 [65536, 5120], P(('dp', 'expert'))
- rope_grad: float32 [64, 5120], P(None, 'expert')
The draws below stay inside these ranges and needn't reach their ends.
Inputs may be any that keep to these rules, and one draw needn't show every extreme that they name: `routes`: each token names 6 different experts.
All inputs are finite; a program needn't handle non-finite values.
Results may differ from the reference program's by a relative error of at most 0.0017.
Values may be sent and summed in bfloat16 or wider, within the bound.
No kernel may reach another device: no remote copies, remote signals or barrier semaphores. Data moves between devices by JAX's collectives and lax.ppermute only.
A program may use at most 64 MiB of HBM per device.

```python
import math
import jax
import jax.numpy as jnp
from jax import lax

D = 5120
FF = 768
TOPK = 6
ROPE = 64
EXP_DEV = 5
TOK_DEV = 128
EXPERTS = 160
WAVE = 32
CAP = 6
BLOCKS = 512
SLOTS = 3072
TOKENS = 65536


def with_spikes(drawn, key, source, target, blocks, factor):
    def block_of(dim):
        return (jnp.arange(drawn.shape[dim]) // (drawn.shape[dim] // blocks)).reshape((-1,) + (1,) * (drawn.ndim - 1 - dim))

    one_side = jax.random.permutation(key, blocks)[block_of(target)]
    second = (block_of(target) + blocks // 2) % blocks
    return jnp.where((block_of(source) == one_side) | (block_of(source) == second), factor * drawn, drawn)


def block_levels(key, dims, cuts, smallest, high):
    def one(position, blocks):
        draws = jax.random.uniform(jax.random.fold_in(jax.random.fold_in(key, 6), position), (blocks,), jnp.float32, smallest / len(cuts), high / len(cuts))
        return jnp.repeat(jnp.exp(draws), dims[position] // blocks).reshape((-1,) + (1,) * (len(dims) - position - 1))

    level = one(*cuts[0])
    for cut in cuts[1:]:
        level = level * one(*cut)
    return level


def choose_distinct(rng, rows, number_of, top, lift):
    sequence = jax.random.permutation(jax.random.fold_in(rng, 1), number_of)
    favour = sequence
    for power in range(3):
        favour = favour * favour // number_of
    favour = favour * lift // number_of
    chance = jax.random.randint(jax.random.fold_in(rng, 2), (rows, number_of), 0, 4096) + favour
    sure = jax.random.permutation(jax.random.fold_in(rng, 3), rows)[jnp.arange(number_of) % rows]
    chance = jnp.where(jnp.arange(rows)[:, None] == sure[None, :], 1 << 14, chance)
    merit = chance * number_of + jnp.arange(number_of)
    return lax.top_k(merit.astype(jnp.int32), top)[1].astype(jnp.int32)


def scatter_about(own_key, shape, scale, reach, cuts=(), kind=jnp.bfloat16):
    gain = block_levels(own_key, shape, cuts, -0.22, 0.18) if cuts else 1.0
    values = jax.random.normal(own_key, shape, jnp.float32) * scale * gain
    return jnp.minimum(jnp.maximum(values, -reach), reach).astype(kind)


def bell_draw_with(stream_key, dims, deviation, reach, split, heavy, kind=jnp.bfloat16):
    result = deviation * jax.random.normal(stream_key, dims, jnp.float32)
    if split:
        result = result * block_levels(stream_key, dims, split, -0.22, 0.18)
    return jnp.clip(with_spikes(result, jax.random.fold_in(stream_key, 3), *heavy), -reach, reach).astype(kind)


def setup_inputs(seed: int = 0) -> dict:
    arg_keys = jax.random.split(jax.random.key(seed), 8)
    routes = choose_distinct(arg_keys[0], TOKENS, EXPERTS, TOPK, 614)
    route_weights = jnp.clip(jnp.exp(math.log(0.5) - 3.218876 * jax.random.uniform(arg_keys[1], (TOKENS, TOPK), jnp.float32) ** block_levels(arg_keys[1], (TOKENS, TOPK), ((0, 512),), -0.2, 0.2)), 0.02, 0.5)
    hidden_grads = scatter_about(arg_keys[2], (WAVE, SLOTS, 2 * FF), 1.0, 6.0, ((0, 32), (1, 16)))
    expert_weight = scatter_about(arg_keys[3], (WAVE, D, 2 * FF), (2 * FF) ** -0.5, 0.15625, ((0, 32), (1, 16)))
    normed = bell_draw_with(arg_keys[4], (TOKENS, D), 1.0, 24.0, ((0, 512),), (0, 1, 512, 6.0))
    key_grad = scatter_about(arg_keys[5], (TOKENS, ROPE), 1.0, 6.0, ((0, 512),))
    rope_weight = scatter_about(arg_keys[6], (ROPE, D), ROPE ** -0.5, 0.75)
    return {"routes": routes, "route_weights": route_weights, "hidden_grads": hidden_grads, "expert_weight": expert_weight, "normed": normed, "key_grad": key_grad, "rope_weight": rope_weight}


def combine_matrix(block_routes, block_weights, experts_here, capacity):
    inside = (block_routes % EXP_DEV) == 0
    column = block_routes // EXP_DEV
    chosen = ((column[:, None] == jnp.arange(experts_here, dtype=jnp.int32)[None, :]) & inside[:, None]).astype(jnp.int32)
    earlier = jnp.cumsum(chosen, axis=0) - chosen
    slot = jnp.sum(earlier * chosen, axis=1)
    kept = inside & (slot < capacity)
    target = column * capacity + slot
    places = (target[:, None] == jnp.arange(experts_here * capacity, dtype=jnp.int32)[None, :]) & kept[:, None]
    weighted = jnp.where(places, block_weights[:, None], jnp.float32(0.0))
    tokens_here = block_routes.shape[0] // TOPK
    return weighted.reshape(tokens_here, TOPK, experts_here * capacity).sum(axis=1).astype(jnp.bfloat16)


def reference(routes, route_weights, hidden_grads, expert_weight, normed, key_grad, rope_weight):
    weight_wide = expert_weight.astype(jnp.float32)
    grouped = jnp.swapaxes(hidden_grads.reshape(WAVE, BLOCKS, CAP, 2 * FF), 0, 1)
    block_routes = routes.reshape(BLOCKS, TOK_DEV * TOPK)
    block_weights = route_weights.reshape(BLOCKS, TOK_DEV * TOPK)

    def one_block(inputs):
        rows, these_routes, these_weights = inputs
        expert_out = jnp.einsum("csf,cdf->csd", rows.astype(jnp.float32), weight_wide).astype(jnp.bfloat16)
        combine = combine_matrix(these_routes, these_weights, WAVE, CAP)
        return jnp.dot(combine, expert_out.reshape(WAVE * CAP, D), preferred_element_type=jnp.float32)

    routed = lax.map(one_block, (grouped, block_routes, block_weights)).reshape(TOKENS, D)
    attention = jnp.dot(key_grad, rope_weight, preferred_element_type=jnp.float32)
    token_grad = (routed + attention).astype(jnp.bfloat16)
    rope_grad = jnp.dot(key_grad.T, normed, preferred_element_type=jnp.float32) * (TOKENS ** -0.5)
    return token_grad, rope_grad
```

```python
import jax
import jax.numpy as jnp
from jax import lax
from jax.sharding import Mesh
from jax.sharding import PartitionSpec as P

TOPK = 6
EXP_DEV = 5
PAD = 8

DP = ("ylo", "z")
EXPERT = ("x", "yhi", "core")
ALL = DP + EXPERT
PLANE = ("ylo",) + EXPERT


def combine_matrix(block_routes, block_weights, experts_here, capacity):
    inside = block_routes % EXP_DEV == 0
    column = block_routes // EXP_DEV
    chosen = (
        (column[:, None] == jnp.arange(experts_here, dtype=jnp.int32)[None, :]) & inside[:, None]
    ).astype(jnp.int32)
    earlier = jnp.cumsum(chosen, axis=0) - chosen
    slot = jnp.sum(earlier * chosen, axis=1)
    kept = inside & (slot < capacity)
    target = column * PAD + slot
    places = (
        target[:, None] == jnp.arange(experts_here * PAD, dtype=jnp.int32)[None, :]
    ) & kept[:, None]
    weighted = jnp.where(places, block_weights[:, None], jnp.float32(0.0))
    tokens_here = block_routes.shape[0] // TOPK
    return (
        weighted.reshape(tokens_here, TOPK, experts_here * PAD)
        .sum(axis=1)
        .astype(jnp.bfloat16)
    )


def body(routes, route_weights, hidden_grads, expert_weight, normed, key_grad, rope_weight):
    groups = lax.axis_size(DP)
    experts_here = lax.axis_size(EXPERT)
    pairs = lax.axis_size("ylo")
    slot_rows = hidden_grads[0]
    projection = expert_weight[0]
    depth = slot_rows.shape[1]
    capacity = slot_rows.shape[0] // experts_here
    width = projection.shape[0] * groups

    partial_grad = lax.dot_general(
        normed, key_grad, (((0,), (0,)), ((), ())), preferred_element_type=jnp.float32
    )
    scale_factor = (key_grad.shape[0] * groups * experts_here) ** (-0.5)
    mine = lax.psum_scatter(partial_grad, EXPERT, scatter_dimension=0, tiled=True)
    terms = lax.all_gather(mine, DP, axis=0)
    rope_grad = jnp.sum(terms, axis=0).T * scale_factor

    other = lax.ppermute(slot_rows, "ylo", [(0, 1), (1, 0)])
    low = lax.axis_index("ylo") == 0
    both = jnp.stack([jnp.where(low, slot_rows, other), jnp.where(low, other, slot_rows)])
    both = both.reshape(pairs * experts_here, capacity, depth)
    both = jnp.pad(both, ((0, 0), (0, PAD - capacity), (0, 0)))
    both = both.reshape(pairs * experts_here * PAD, depth)
    gathered = lax.all_gather(projection, "z", axis=0, tiled=True)
    product = lax.dot_general(
        both, gathered, (((1,), (1,)), ((), ())), preferred_element_type=jnp.float32
    )
    computed = product.astype(jnp.bfloat16).reshape(pairs * experts_here, PAD, -1)
    returned = lax.all_to_all(computed, PLANE, split_axis=0, concat_axis=0, tiled=True)
    returned = returned.reshape(pairs, experts_here * PAD, -1)
    combine = combine_matrix(routes.reshape(-1), route_weights.reshape(-1), experts_here, capacity)
    routed = jnp.concatenate(
        [jnp.dot(combine, returned[g], preferred_element_type=jnp.float32) for g in range(pairs)],
        axis=1,
    )
    attention = jnp.dot(key_grad, rope_weight, preferred_element_type=jnp.float32)
    token_grad = (routed + attention).astype(jnp.bfloat16)
    return (token_grad, rope_grad)


def solution(mesh):
    wide = Mesh(mesh.devices.reshape(2, 8, 4, 4, 2), ALL)
    return jax.shard_map(
        body,
        mesh=wide,
        in_specs=(
            P(ALL, None),
            P(ALL, None),
            P(EXPERT, DP, None),
            P(EXPERT, DP, None),
            P(ALL, None),
            P(ALL, None),
            P(),
        ),
        out_specs=(P(ALL, None), P(None, EXPERT)),
        check_vma=False,
    )
```

```python
import functools

import jax
import jax.numpy as jnp
from jax import lax
from jax.experimental import pallas as pl
from jax.experimental.pallas import tpu as pltpu
from jax.sharding import Mesh
from jax.sharding import PartitionSpec as P

EXP_DEV = 5
PAD = 8

DP = ("ylo", "z")
EXPERT = ("x", "yhi", "core")
ALL = DP + EXPERT
PLANE = ("ylo",) + EXPERT

VMEM = pl.BlockSpec(memory_space=pltpu.VMEM)
SMEM = pl.BlockSpec(memory_space=pltpu.SMEM)


def call(kernel, out_shape, in_specs, flops, moved, scratch=(), after=()):
    taken = len(in_specs)

    def without(*refs):
        kernel(*refs[:taken], *refs[taken + len(after) :])

    run = pl.pallas_call(
        without,
        out_shape=out_shape,
        in_specs=list(in_specs) + [pl.BlockSpec(memory_space=pl.ANY)] * len(after),
        out_specs=jax.tree.map(lambda _: VMEM, out_shape),
        scratch_shapes=list(scratch),
        compiler_params=pltpu.CompilerParams(vmem_limit_bytes=32 * 1024 * 1024),
        cost_estimate=pl.CostEstimate(flops=flops, bytes_accessed=moved, transcendentals=0),
    )
    return lambda *args: run(*args, *after)


def struct(shape, dtype):
    return jax.ShapeDtypeStruct(shape, dtype)


def partial_kernel(order, normed_ref, key_ref, out_ref):
    product = lax.dot_general(
        key_ref[...], normed_ref[...], (((0,), (0,)), ((), ())), preferred_element_type=jnp.float32
    )
    key, width = product.shape
    share = width // len(order)
    rest = share - 128
    group = key * rest // 128
    rows = key + group
    for e, place in enumerate(order):
        out_ref[place * rows : place * rows + key, :] = product[:, e * share : e * share + 128]
        tail = product[:, e * share + 128 : (e + 1) * share]
        out_ref[place * rows + key : (place + 1) * rows, :] = jnp.concatenate(
            [tail[a * group : (a + 1) * group] for a in range(key // group)], axis=1
        )


def rope_kernel(key, share, scale_factor, total_ref, out_ref):
    total = total_ref[...] * scale_factor
    rest = share - 128
    tail = jnp.concatenate([total[key:, a * rest : (a + 1) * rest] for a in range(128 // rest)], axis=0)
    out_ref[...] = jnp.concatenate([total[:key, :], tail], axis=1)


def combine_kernel(experts, capacity, routes_ref, weights_ref, out_ref):
    tokens, topk = routes_ref.shape
    expert = lax.broadcasted_iota(jnp.int32, (tokens, experts), 1)
    chosen = jnp.zeros((tokens, experts), jnp.float32)
    weight = jnp.zeros((tokens, experts), jnp.float32)
    for k in range(topk):
        here = routes_ref[:, k : k + 1] == expert * EXP_DEV
        chosen = jnp.where(here, 1.0, chosen)
        weight = jnp.where(here, weights_ref[:, k : k + 1], weight)
    row = lax.broadcasted_iota(jnp.int32, (tokens, tokens), 0)
    column = lax.broadcasted_iota(jnp.int32, (tokens, tokens), 1)
    before = (column < row).astype(jnp.bfloat16)
    slot = jnp.dot(before, chosen.astype(jnp.bfloat16), preferred_element_type=jnp.float32)
    slot = jnp.where(chosen > 0.0, slot, 128.0)
    spread = (
        lax.broadcasted_iota(jnp.int32, (experts, experts * PAD), 1) // PAD
        == lax.broadcasted_iota(jnp.int32, (experts, experts * PAD), 0)
    ).astype(jnp.bfloat16)
    slots = jnp.dot(slot.astype(jnp.bfloat16), spread, preferred_element_type=jnp.float32)
    weights = jnp.dot(weight.astype(jnp.bfloat16), spread, preferred_element_type=jnp.float32)
    place = lax.rem(lax.broadcasted_iota(jnp.int32, slots.shape, 1), PAD)
    kept = (slots == place.astype(jnp.float32)) & (place < capacity)
    out_ref[...] = jnp.where(kept, weights, 0.0).astype(out_ref.dtype)


def rows_kernel(capacity, low_ref, own_ref, other_ref, out_ref):
    own, other = own_ref[...], other_ref[...]
    low = low_ref[0] == 1
    rows, depth = own.shape
    empty = jnp.zeros((rows // capacity, PAD - capacity, depth), own.dtype)
    for g, part in enumerate((jnp.where(low, own, other), jnp.where(low, other, own))):
        spaced = jnp.concatenate([part.reshape(rows // capacity, capacity, depth), empty], axis=1)
        out_ref[g] = spaced.reshape(rows // capacity * PAD, depth)


def products_kernel(capacity, rows_ref, *refs):
    weights, (out_ref, lines_ref) = refs[:-2], refs[-2:]
    targets, lines, lanes = out_ref.shape
    products = [
        lax.dot_general(
            rows_ref[...], ref[...], (((1,), (1,)), ((), ())), preferred_element_type=jnp.float32
        )
        for ref in weights
    ]
    width = sum(product.shape[1] for product in products)
    blocks = -(-width // lanes)
    if blocks * lanes > width:
        products.append(jnp.zeros((targets * PAD, blocks * lanes - width), jnp.float32))
    product = jnp.concatenate(products, axis=1).reshape(targets, PAD, blocks * lanes)
    for j in range(blocks):
        lines_ref[:, j * capacity : (j + 1) * capacity, :] = product[
            :, :capacity, j * lanes : (j + 1) * lanes
        ]
    if lines > blocks * capacity:
        lines_ref[:, blocks * capacity :, :] = jnp.zeros(
            (targets, lines - blocks * capacity, lanes), jnp.float32
        )
    out_ref[...] = lines_ref[...].astype(out_ref.dtype)


def routed_sums(capacity, combine, chunk_ref, lines_ref):
    targets, lines, lanes = chunk_ref.shape
    blocks = lines // capacity
    lines_ref[:, :lines, :] = chunk_ref[...].astype(jnp.float32)
    lines_ref[:, lines : lines + PAD, :] = jnp.zeros((targets, PAD, lanes), jnp.float32)
    columns = [
        lines_ref[:, j * capacity : j * capacity + PAD, :].reshape(targets * PAD, lanes)
        for j in range(blocks)
    ]
    rows = jnp.concatenate(columns, axis=1).astype(jnp.bfloat16)
    half = combine.shape[1]
    return [
        jnp.dot(combine, rows[g * half : (g + 1) * half], preferred_element_type=jnp.float32)
        for g in range(rows.shape[0] // half)
    ]


def halves_kernel(half, low_ref, high_ref, low_out, high_out):
    low_out[...] = low_ref[:half, :]
    high_out[...] = high_ref[half:, :]


def early_kernel(capacity, layout, late, z_ref, combine_ref, key_ref, rope_ref, *refs):
    chunks, (held_ref, rest_ref, attention_ref, lines_ref) = refs[:-4], refs[-4:]
    groups, tokens, piece = attention_ref.shape
    pairs, ring = held_ref.shape[:2]
    attention = jnp.dot(key_ref[...], rope_ref[...], preferred_element_type=jnp.float32)
    for d in range(groups):
        attention_ref[d] = attention[:, d * piece : (d + 1) * piece]
    z = z_ref[0]

    def here(g, distance):
        return attention_ref[g * ring + lax.rem(z + distance + ring, ring)]

    for chunk, distances in zip(chunks, layout):
        for g, routed in enumerate(routed_sums(capacity, combine_ref[...], chunk, lines_ref)):
            for i, distance in enumerate(distances):
                held_ref[g, distance % ring] = (
                    routed[:, i * piece : (i + 1) * piece] + here(g, distance)
                ).astype(held_ref.dtype)
    for g in range(pairs):
        for i, distance in enumerate(late):
            held_ref[g, distance % ring] = jnp.zeros((tokens, piece), held_ref.dtype)
            rest_ref[g, i] = here(g, distance)


def late_kernel(
    capacity, distances, early, z_ref, combine_ref, chunk_ref, held_ref, rest_ref, out_ref, pieces_ref, lines_ref
):
    pairs, ring, tokens, piece = held_ref.shape
    z = z_ref[0]
    for g, routed in enumerate(routed_sums(capacity, combine_ref[...], chunk_ref, lines_ref)):
        for distance in early:
            pieces_ref[distance % ring] = held_ref[g, distance % ring]
        for i, distance in enumerate(distances):
            pieces_ref[distance % ring] = (
                routed[:, i * piece : (i + 1) * piece] + rest_ref[g, i]
            ).astype(pieces_ref.dtype)
        for h in range(ring // 2):
            left = pieces_ref[lax.rem(2 * h - z + ring, ring)]
            right = pieces_ref[lax.rem(2 * h + 1 - z + ring, ring)]
            columns = slice((g * ring + 2 * h) * piece, (g * ring + 2 * h + 2) * piece)
            out_ref[:, columns] = jnp.concatenate([left, right], axis=1)


def body(routes, route_weights, hidden_grads, expert_weight, normed, key_grad, rope_weight):
    groups = lax.axis_size(DP)
    experts_here = lax.axis_size(EXPERT)
    pairs = lax.axis_size("ylo")
    ring = lax.axis_size("z")
    slot_rows = hidden_grads[0]
    projection = expert_weight[0]
    depth = slot_rows.shape[1]
    capacity = slot_rows.shape[0] // experts_here
    piece = projection.shape[0]
    tokens, key_size = key_grad.shape
    width = piece * groups
    share = width // experts_here
    last = ring // 2
    rows = experts_here * PAD
    z = lax.axis_index("z").astype(jnp.int32).reshape(1)
    low = (lax.axis_index("ylo") == 0).astype(jnp.int32).reshape(1)
    up = [(i, (i + 1) % ring) for i in range(ring)]
    down = [(i, (i - 1) % ring) for i in range(ring)]

    packed = key_size * share // 128
    columns, cores = lax.axis_size("yhi"), lax.axis_size("core")
    order = tuple(
        (e // (columns * cores) * cores + e % cores) * columns + e // cores % columns
        for e in range(experts_here)
    )
    partial_grad = call(
        functools.partial(partial_kernel, order),
        struct((experts_here * packed, 128), jnp.float32),
        [VMEM, VMEM],
        2 * tokens * key_size * width,
        3 * 10**6,
    )(normed, key_grad)
    mine = lax.psum_scatter(partial_grad, ("x", "core"), scatter_dimension=0, tiled=True)

    slot_rows, partial_grad = lax.optimization_barrier((slot_rows, partial_grad))
    other = lax.ppermute(slot_rows, "ylo", [(0, 1), (1, 0)])

    def spaced_rows(other):
        return call(
            functools.partial(rows_kernel, capacity),
            struct((pairs, rows, depth), jnp.bfloat16),
            [SMEM, VMEM, VMEM],
            0,
            3 * 10**6,
        )(low, slot_rows, other).reshape(pairs * rows, depth)

    def products(weights, flops, after=()):
        columns = sum(w.shape[0] for w in weights)
        lines = -(-(-(-columns // 128) * capacity) // 16) * 16
        shape = (pairs * experts_here, lines, 128)
        return call(
            functools.partial(products_kernel, capacity),
            struct(shape, jnp.bfloat16),
            [VMEM] * (1 + len(weights)),
            flops,
            4 * 10**6,
            [pltpu.VMEM(shape, jnp.float32)],
            after,
        )(both, *weights)

    def send(computed):
        return lax.all_to_all(computed, PLANE, split_axis=0, concat_axis=0, tiled=True)

    layout = ((0, -1, 1), (-2, 2), (-3, 3, 4))
    below, above = [projection], [projection]
    below.append(lax.ppermute(below[-1], "z", up))
    above.append(lax.ppermute(above[-1], "z", down))
    below[1], other = lax.optimization_barrier((below[1], other))
    both = spaced_rows(other)
    first = products([projection, below[1], above[1]], 25 * 10**9)
    below.append(lax.ppermute(below[-1], "z", up))
    above.append(lax.ppermute(above[-1], "z", down))
    below[2], _, mine = lax.optimization_barrier((below[2], first, mine))
    second = products([below[2], above[2]], 25 * 10**9)
    below.append(lax.ppermute(below[-1], "z", up))
    above.append(lax.ppermute(above[-1], "z", down))
    sent = [send(first)]
    half = piece // 2
    half_low, half_high = call(
        functools.partial(halves_kernel, half),
        [struct((half, depth), jnp.bfloat16)] * 2,
        [VMEM] * 2,
        0,
        3 * 10**6,
        after=[second] + sent,
    )(below[-1], above[-1])
    last_low = lax.ppermute(half_low, "z", up)
    last_high = lax.ppermute(half_high, "z", down)
    sent.append(send(second))
    terms = lax.all_gather(mine, ("yhi", "ylo"), axis=0, tiled=True)
    terms = terms.reshape(columns * pairs, columns, packed, 128)
    summed = jnp.sum(lax.dynamic_index_in_dim(terms, lax.axis_index("yhi"), 1, False), axis=0)
    third = products([below[3], above[3], last_low, last_high], 15 * 10**9, [summed] + sent[1:])
    chunks = sent + [send(third)]

    bit = 1
    while bit < ring:
        summed = summed + lax.ppermute(summed, "z", [(i, i ^ bit) for i in range(ring)])
        bit *= 2
    scale_factor = (tokens * groups * experts_here) ** (-0.5)
    rope_grad = call(
        functools.partial(rope_kernel, key_size, share, scale_factor),
        struct((key_size, share), jnp.float32),
        [VMEM],
        0,
        10**6,
    )(summed)

    combine = call(
        functools.partial(combine_kernel, experts_here, capacity),
        struct((tokens, rows), jnp.bfloat16),
        [VMEM, VMEM],
        10**7,
        10**6,
    )(routes, route_weights)
    most = max(chunk.shape[1] for chunk in chunks)
    lines = pltpu.VMEM((pairs * experts_here, most + PAD, 128), jnp.float32)
    held, rest = call(
        functools.partial(early_kernel, capacity, layout[:-1], layout[-1]),
        [
            struct((pairs, ring, tokens, piece), jnp.bfloat16),
            struct((pairs, len(layout[-1]), tokens, piece), jnp.float32),
        ],
        [SMEM] + [VMEM] * (3 + len(chunks[:-1])),
        4 * 10**8,
        8 * 10**6,
        [pltpu.VMEM((groups, tokens, piece), jnp.float32), lines],
    )(z, combine, key_grad, rope_weight, *chunks[:-1])
    token_grad = call(
        functools.partial(late_kernel, capacity, layout[-1], sum(layout[:-1], ())),
        struct((tokens, width), jnp.bfloat16),
        [SMEM] + [VMEM] * 4,
        4 * 10**7,
        3 * 10**6,
        [pltpu.VMEM((ring, tokens, piece), jnp.bfloat16), lines],
    )(z, combine, chunks[-1], held, rest)
    return (token_grad, rope_grad)


def solution(mesh):
    wide = Mesh(mesh.devices.reshape(2, 8, 4, 4, 2), ALL)
    return jax.shard_map(
        body,
        mesh=wide,
        in_specs=(
            P(ALL, None),
            P(ALL, None),
            P(EXPERT, DP, None),
            P(EXPERT, DP, None),
            P(ALL, None),
            P(ALL, None),
            P(),
        ),
        out_specs=(P(ALL, None), P(None, EXPERT)),
        check_vma=False,
    )
```

```python
import functools

import jax
import jax.numpy as jnp
from jax import lax
from jax.experimental import pallas as pl
from jax.experimental.pallas import tpu as pltpu
from jax.sharding import Mesh
from jax.sharding import PartitionSpec as P

EXP_DEV = 5
PAD = 8

DP = ("ylo", "z")
EXPERT = ("x", "yhi", "core")
ALL = DP + EXPERT
PLANE = ("ylo",) + EXPERT

VMEM = pl.BlockSpec(memory_space=pltpu.VMEM)
SMEM = pl.BlockSpec(memory_space=pltpu.SMEM)


def call(kernel, out_shape, in_specs, flops, moved, scratch=(), after=()):
    taken = len(in_specs)

    def without(*refs):
        kernel(*refs[:taken], *refs[taken + len(after) :])

    run = pl.pallas_call(
        without,
        out_shape=out_shape,
        in_specs=list(in_specs) + [pl.BlockSpec(memory_space=pl.ANY)] * len(after),
        out_specs=jax.tree.map(lambda _: VMEM, out_shape),
        scratch_shapes=list(scratch),
        compiler_params=pltpu.CompilerParams(vmem_limit_bytes=16 * 1024 * 1024),
        cost_estimate=pl.CostEstimate(flops=flops, bytes_accessed=moved, transcendentals=0),
    )
    return lambda *args: run(*args, *after)


def struct(shape, dtype):
    return jax.ShapeDtypeStruct(shape, dtype)


def partial_kernel(places, core_ref, normed_ref, key_ref, other_normed_ref, other_key_ref, out_ref):
    dims = (((0,), (0,)), ((), ()))
    product = lax.dot_general(
        key_ref[...], normed_ref[...], dims, preferred_element_type=jnp.float32
    ) + lax.dot_general(
        other_key_ref[...], other_normed_ref[...], dims, preferred_element_type=jnp.float32
    )
    key, width = product.shape
    share = width // (2 * len(places))
    rest = share - 128
    group = key * rest // 128
    first = core_ref[0] == 0
    for place, (low, high) in enumerate(places):
        part = jnp.where(
            first,
            product[:, low * share : (low + 1) * share],
            product[:, high * share : (high + 1) * share],
        )
        out_ref[place, :key, :] = part[:, :128]
        out_ref[place, key:, :] = jnp.concatenate(
            [part[a * group : (a + 1) * group, 128:] for a in range(key // group)], axis=1
        )


def rope_kernel(key, share, scale_factor, total_ref, out_ref):
    total = total_ref[...] * scale_factor
    rest = share - 128
    tail = jnp.concatenate([total[key:, a * rest : (a + 1) * rest] for a in range(128 // rest)], axis=0)
    out_ref[...] = jnp.concatenate([total[:key, :], tail], axis=1)


def combine_kernel(experts, capacity, routes_ref, weights_ref, out_ref):
    tokens, topk = routes_ref.shape
    expert = lax.broadcasted_iota(jnp.int32, (tokens, experts), 1)
    chosen = jnp.zeros((tokens, experts), jnp.float32)
    weight = jnp.zeros((tokens, experts), jnp.float32)
    for k in range(topk):
        here = routes_ref[:, k : k + 1] == expert * EXP_DEV
        chosen = jnp.where(here, 1.0, chosen)
        weight = jnp.where(here, weights_ref[:, k : k + 1], weight)
    row = lax.broadcasted_iota(jnp.int32, (tokens, tokens), 0)
    column = lax.broadcasted_iota(jnp.int32, (tokens, tokens), 1)
    before = (column < row).astype(jnp.bfloat16)
    slot = jnp.dot(before, chosen.astype(jnp.bfloat16), preferred_element_type=jnp.float32)
    slot = jnp.where(chosen > 0.0, slot, 128.0)
    spread = (
        lax.broadcasted_iota(jnp.int32, (experts, experts * PAD), 1) // PAD
        == lax.broadcasted_iota(jnp.int32, (experts, experts * PAD), 0)
    ).astype(jnp.bfloat16)
    slots = jnp.dot(slot.astype(jnp.bfloat16), spread, preferred_element_type=jnp.float32)
    weights = jnp.dot(weight.astype(jnp.bfloat16), spread, preferred_element_type=jnp.float32)
    place = lax.rem(lax.broadcasted_iota(jnp.int32, slots.shape, 1), PAD)
    kept = (slots == place.astype(jnp.float32)) & (place < capacity)
    out_ref[...] = jnp.where(kept, weights, 0.0).astype(out_ref.dtype)


def rows_kernel(capacity, low_ref, own_ref, other_ref, out_ref):
    own, other = own_ref[...], other_ref[...]
    low = low_ref[0] == 1
    rows, depth = own.shape
    empty = jnp.zeros((rows // capacity, PAD - capacity, depth), own.dtype)
    for g, part in enumerate((jnp.where(low, own, other), jnp.where(low, other, own))):
        spaced = jnp.concatenate([part.reshape(rows // capacity, capacity, depth), empty], axis=1)
        out_ref[g] = spaced.reshape(rows // capacity * PAD, depth)


def put_lines(capacity, rows_ref, weights, lines_ref, start, end):
    targets, _, lanes = lines_ref.shape
    products = [
        lax.dot_general(
            rows_ref[...], ref[...], (((1,), (1,)), ((), ())), preferred_element_type=jnp.float32
        )
        for ref in weights
    ]
    width = sum(product.shape[1] for product in products)
    blocks = -(-width // lanes)
    if blocks * lanes > width:
        products.append(jnp.zeros((targets * PAD, blocks * lanes - width), jnp.float32))
    product = jnp.concatenate(products, axis=1).reshape(targets, PAD, blocks * lanes)
    for j in range(blocks):
        lines_ref[:, start + j * capacity : start + (j + 1) * capacity, :] = product[
            :, :capacity, j * lanes : (j + 1) * lanes
        ]
    done = start + blocks * capacity
    if end > done:
        lines_ref[:, done:end, :] = jnp.zeros((targets, end - done, lanes), jnp.float32)


def products_kernel(capacity, rows_ref, *refs):
    weights, (out_ref, lines_ref) = refs[:-2], refs[-2:]
    put_lines(capacity, rows_ref, weights, lines_ref, 0, out_ref.shape[1])
    out_ref[...] = lines_ref[...].astype(out_ref.dtype)


def routed_sums(capacity, combine, chunk_ref, lines_ref):
    targets, lines, lanes = chunk_ref.shape
    blocks = lines // capacity
    lines_ref[:, :lines, :] = chunk_ref[...].astype(jnp.float32)
    lines_ref[:, lines : lines + PAD, :] = jnp.zeros((targets, PAD, lanes), jnp.float32)
    columns = [
        lines_ref[:, j * capacity : j * capacity + PAD, :].reshape(targets * PAD, lanes)
        for j in range(blocks)
    ]
    rows = jnp.concatenate(columns, axis=1).astype(jnp.bfloat16)
    half = combine.shape[1]
    return [
        jnp.dot(combine, rows[g * half : (g + 1) * half], preferred_element_type=jnp.float32)
        for g in range(rows.shape[0] // half)
    ]


def more_products_kernel(capacity, rows_ref, begun_ref, *refs):
    weights, (out_ref, lines_ref) = refs[:-2], refs[-2:]
    targets, lines, lanes = out_ref.shape
    held = begun_ref.shape[1] // capacity * capacity
    lines_ref[:, : begun_ref.shape[1], :] = begun_ref[...].astype(jnp.float32)
    put_lines(capacity, rows_ref, weights, lines_ref, held, lines)
    out_ref[...] = lines_ref[...].astype(out_ref.dtype)


def halves_kernel(half, low_ref, high_ref, low_out, high_out):
    low_out[...] = low_ref[:half, :]
    high_out[...] = high_ref[half:, :]


def early_kernel(capacity, layout, late, z_ref, combine_ref, key_ref, rope_ref, *refs):
    chunks, (held_ref, rest_ref, attention_ref, lines_ref) = refs[:-4], refs[-4:]
    groups, tokens, piece = attention_ref.shape
    pairs, ring = held_ref.shape[:2]
    attention = jnp.dot(key_ref[...], rope_ref[...], preferred_element_type=jnp.float32)
    for d in range(groups):
        attention_ref[d] = attention[:, d * piece : (d + 1) * piece]
    z = z_ref[0]

    def here(g, distance):
        return attention_ref[g * ring + lax.rem(z + distance + ring, ring)]

    for chunk, distances in zip(chunks, layout):
        for g, routed in enumerate(routed_sums(capacity, combine_ref[...], chunk, lines_ref)):
            for i, distance in enumerate(distances):
                held_ref[g, distance % ring] = (
                    routed[:, i * piece : (i + 1) * piece] + here(g, distance)
                ).astype(held_ref.dtype)
    for g in range(pairs):
        for i, distance in enumerate(late):
            held_ref[g, distance % ring] = jnp.zeros((tokens, piece), held_ref.dtype)
            rest_ref[g, i] = here(g, distance)


def late_kernel(
    capacity, distances, early, z_ref, combine_ref, chunk_ref, held_ref, rest_ref, out_ref, pieces_ref, lines_ref
):
    pairs, ring, tokens, piece = held_ref.shape
    z = z_ref[0]
    for g, routed in enumerate(routed_sums(capacity, combine_ref[...], chunk_ref, lines_ref)):
        for distance in early:
            pieces_ref[distance % ring] = held_ref[g, distance % ring]
        for i, distance in enumerate(distances):
            pieces_ref[distance % ring] = (
                routed[:, i * piece : (i + 1) * piece] + rest_ref[g, i]
            ).astype(pieces_ref.dtype)
        for h in range(ring // 2):
            left = pieces_ref[lax.rem(2 * h - z + ring, ring)]
            right = pieces_ref[lax.rem(2 * h + 1 - z + ring, ring)]
            columns = slice((g * ring + 2 * h) * piece, (g * ring + 2 * h + 2) * piece)
            out_ref[:, columns] = jnp.concatenate([left, right], axis=1)


def body(routes, route_weights, hidden_grads, expert_weight, normed, key_grad, rope_weight):
    groups = lax.axis_size(DP)
    experts_here = lax.axis_size(EXPERT)
    pairs = lax.axis_size("ylo")
    ring = lax.axis_size("z")
    slot_rows = hidden_grads[0]
    projection = expert_weight[0]
    depth = slot_rows.shape[1]
    capacity = slot_rows.shape[0] // experts_here
    piece = projection.shape[0]
    tokens, key_size = key_grad.shape
    width = piece * groups
    share = width // experts_here
    last = ring // 2
    rows = experts_here * PAD
    z = lax.axis_index("z").astype(jnp.int32).reshape(1)
    low = (lax.axis_index("ylo") == 0).astype(jnp.int32).reshape(1)
    up = [(i, (i + 1) % ring) for i in range(ring)]
    down = [(i, (i - 1) % ring) for i in range(ring)]

    packed = key_size * share // 128
    cores = lax.axis_size("core")
    places = tuple(
        tuple(place * cores + core for core in range(cores)) for place in range(experts_here // cores)
    )
    swap = [(0, 1), (1, 0)]
    mine = call(
        functools.partial(partial_kernel, places),
        struct((len(places), packed, 128), jnp.float32),
        [SMEM] + [VMEM] * 4,
        4 * tokens * key_size * width,
        4 * 10**6,
    )(
        lax.axis_index("core").astype(jnp.int32).reshape(1),
        normed,
        key_grad,
        lax.ppermute(normed, "core", swap),
        lax.ppermute(key_grad, "core", swap),
    )
    terms = lax.all_to_all(mine, ("x", "yhi"), split_axis=0, concat_axis=0, tiled=True)
    mine = jnp.sum(terms, axis=0)

    other = lax.ppermute(slot_rows, "ylo", swap)

    def spaced_rows(other):
        return call(
            functools.partial(rows_kernel, capacity),
            struct((pairs, rows, depth), jnp.bfloat16),
            [SMEM, VMEM, VMEM],
            0,
            3 * 10**6,
        )(low, slot_rows, other).reshape(pairs * rows, depth)

    def products(weights, flops, after=()):
        columns = sum(w.shape[0] for w in weights)
        lines = -(-(-(-columns // 128) * capacity) // 16) * 16
        shape = (pairs * experts_here, lines, 128)
        return call(
            functools.partial(products_kernel, capacity),
            struct(shape, jnp.bfloat16),
            [VMEM] * (1 + len(weights)),
            flops,
            4 * 10**6,
            [pltpu.VMEM(shape, jnp.float32)],
            after,
        )(both, *weights)

    def added(sums, bit):
        return sums + lax.ppermute(sums, "z", [(i, i ^ bit) for i in range(ring)])

    def send(computed):
        return lax.all_to_all(computed, PLANE, split_axis=0, concat_axis=0, tiled=True)

    layout = ((0, -1, 1), (-2, 2), (-3, 3, 4))
    below, above = [projection], [projection]
    below.append(lax.ppermute(below[-1], "z", up))
    above.append(lax.ppermute(above[-1], "z", down))
    below[1], above[1], other = lax.optimization_barrier((below[1], above[1], other))
    both = spaced_rows(other)
    first = products([projection, below[1], above[1]], 2 * 10**9)
    first, mine = lax.optimization_barrier((first, mine))
    below.append(lax.ppermute(below[-1], "z", up))
    above.append(lax.ppermute(above[-1], "z", down))
    below[2], _ = lax.optimization_barrier((below[2], first))
    above[2], _ = lax.optimization_barrier((above[2], first))
    second = products([below[2], above[2]], 25 * 10**9)
    below.append(lax.ppermute(below[-1], "z", up))
    above.append(lax.ppermute(above[-1], "z", down))
    sent = [send(first)]
    half = piece // 2
    half_low, half_high = call(
        functools.partial(halves_kernel, half),
        [struct((half, depth), jnp.bfloat16)] * 2,
        [VMEM] * 2,
        0,
        3 * 10**6,
        after=[second] + sent,
    )(below[-1], above[-1])
    last_low = lax.ppermute(half_low, "z", up)
    last_high = lax.ppermute(half_high, "z", down)
    sent.append(send(second))
    two = added(added(mine, 1), 2)
    begun = products([below[3], above[3]], 10 * 10**9)
    shape = (pairs * experts_here, 48, 128)
    third = call(
        functools.partial(more_products_kernel, capacity),
        struct(shape, jnp.bfloat16),
        [VMEM] * 4,
        1 * 10**9,
        3 * 10**6,
        [pltpu.VMEM(shape, jnp.float32)],
        [two],
    )(both, begun, last_low, last_high)
    chunks = sent + [send(third)]

    combine = call(
        functools.partial(combine_kernel, experts_here, capacity),
        struct((tokens, rows), jnp.bfloat16),
        [VMEM, VMEM],
        10**7,
        10**6,
    )(routes, route_weights)
    most = max(chunk.shape[1] for chunk in chunks)
    lines = pltpu.VMEM((pairs * experts_here, most + PAD, 128), jnp.float32)
    held, rest = call(
        functools.partial(early_kernel, capacity, layout[:-1], layout[-1]),
        [
            struct((pairs, ring, tokens, piece), jnp.bfloat16),
            struct((pairs, len(layout[-1]), tokens, piece), jnp.float32),
        ],
        [SMEM] + [VMEM] * (3 + len(chunks[:-1])),
        4 * 10**8,
        8 * 10**6,
        [pltpu.VMEM((groups, tokens, piece), jnp.float32), lines],
    )(z, combine, key_grad, rope_weight, *chunks[:-1])
    summed = added(two, 4)
    summed = summed + lax.ppermute(summed, "ylo", swap)
    scale_factor = (tokens * groups * experts_here) ** (-0.5)
    rope_grad = call(
        functools.partial(rope_kernel, key_size, share, scale_factor),
        struct((key_size, share), jnp.float32),
        [VMEM],
        0,
        10**6,
    )(summed)

    token_grad = call(
        functools.partial(late_kernel, capacity, layout[-1], sum(layout[:-1], ())),
        struct((tokens, width), jnp.bfloat16),
        [SMEM] + [VMEM] * 4,
        4 * 10**7,
        3 * 10**6,
        [pltpu.VMEM((ring, tokens, piece), jnp.bfloat16), lines],
    )(z, combine, chunks[-1], held, rest)
    return (token_grad, rope_grad)


def solution(mesh):
    wide = Mesh(mesh.devices.reshape(2, 8, 4, 4, 2), ALL)
    return jax.shard_map(
        body,
        mesh=wide,
        in_specs=(
            P(ALL, None),
            P(ALL, None),
            P(EXPERT, DP, None),
            P(EXPERT, DP, None),
            P(ALL, None),
            P(ALL, None),
            P(),
        ),
        out_specs=(P(ALL, None), P(None, EXPERT)),
        check_vma=False,
    )
```

```python
import functools

import jax
import jax.numpy as jnp
from jax import lax
from jax.experimental import pallas as pl
from jax.experimental.pallas import tpu as pltpu
from jax.sharding import Mesh
from jax.sharding import PartitionSpec as P

EXP_DEV = 5
PAD = 8

DP = ("ylo", "z")
EXPERT = ("x", "yhi", "core")
ALL = DP + EXPERT
PLANE = ("ylo",) + EXPERT

VMEM = pl.BlockSpec(memory_space=pltpu.VMEM)
SMEM = pl.BlockSpec(memory_space=pltpu.SMEM)
ANY = pl.BlockSpec(memory_space=pl.ANY)


def call(kernel, out_shape, in_specs, flops, moved, scratch=(), after=(), out_spec=VMEM):
    taken = len(in_specs)

    def without(*refs):
        kernel(*refs[:taken], *refs[taken + len(after) :])

    run = pl.pallas_call(
        without,
        out_shape=out_shape,
        in_specs=list(in_specs) + [ANY] * len(after),
        out_specs=jax.tree.map(lambda _: out_spec, out_shape),
        scratch_shapes=list(scratch),
        compiler_params=pltpu.CompilerParams(vmem_limit_bytes=16 * 1024 * 1024),
        cost_estimate=pl.CostEstimate(flops=flops, bytes_accessed=moved, transcendentals=0),
    )
    return lambda *args: run(*args, *after)


def struct(shape, dtype):
    return jax.ShapeDtypeStruct(shape, dtype)


def partial_kernel(places, core_ref, normed_ref, key_ref, other_normed_ref, other_key_ref, out_ref):
    dims = (((0,), (0,)), ((), ()))
    product = lax.dot_general(
        key_ref[...], normed_ref[...], dims, preferred_element_type=jnp.float32
    ) + lax.dot_general(
        other_key_ref[...], other_normed_ref[...], dims, preferred_element_type=jnp.float32
    )
    key, width = product.shape
    share = width // (2 * len(places))
    rest = share - 128
    group = key * rest // 128
    first = core_ref[0] == 0
    for place, (low, high) in enumerate(places):
        part = jnp.where(
            first,
            product[:, low * share : (low + 1) * share],
            product[:, high * share : (high + 1) * share],
        )
        out_ref[place, :key, :] = part[:, :128]
        out_ref[place, key:, :] = jnp.concatenate(
            [part[a * group : (a + 1) * group, 128:] for a in range(key // group)], axis=1
        )


def rope_kernel(key, share, scale_factor, total_ref, out_ref):
    total = total_ref[...] * scale_factor
    rest = share - 128
    tail = jnp.concatenate([total[key:, a * rest : (a + 1) * rest] for a in range(128 // rest)], axis=0)
    out_ref[...] = jnp.concatenate([total[:key, :], tail], axis=1)


def combine_kernel(experts, capacity, routes_ref, weights_ref, out_ref):
    tokens, topk = routes_ref.shape
    expert = lax.broadcasted_iota(jnp.int32, (tokens, experts), 1)
    chosen = jnp.zeros((tokens, experts), jnp.float32)
    weight = jnp.zeros((tokens, experts), jnp.float32)
    for k in range(topk):
        here = routes_ref[:, k : k + 1] == expert * EXP_DEV
        chosen = jnp.where(here, 1.0, chosen)
        weight = jnp.where(here, weights_ref[:, k : k + 1], weight)
    row = lax.broadcasted_iota(jnp.int32, (tokens, tokens), 0)
    column = lax.broadcasted_iota(jnp.int32, (tokens, tokens), 1)
    before = (column < row).astype(jnp.bfloat16)
    slot = jnp.dot(before, chosen.astype(jnp.bfloat16), preferred_element_type=jnp.float32)
    slot = jnp.where(chosen > 0.0, slot, 128.0)
    spread = (
        lax.broadcasted_iota(jnp.int32, (experts, experts * PAD), 1) // PAD
        == lax.broadcasted_iota(jnp.int32, (experts, experts * PAD), 0)
    ).astype(jnp.bfloat16)
    slots = jnp.dot(slot.astype(jnp.bfloat16), spread, preferred_element_type=jnp.float32)
    weights = jnp.dot(weight.astype(jnp.bfloat16), spread, preferred_element_type=jnp.float32)
    place = lax.rem(lax.broadcasted_iota(jnp.int32, slots.shape, 1), PAD)
    kept = (slots == place.astype(jnp.float32)) & (place < capacity)
    out_ref[...] = jnp.where(kept, weights, 0.0).astype(out_ref.dtype)


def rows_kernel(capacity, low_ref, own_ref, other_ref, out_ref):
    own, other = own_ref[...], other_ref[...]
    low = low_ref[0] == 1
    rows, depth = own.shape
    empty = jnp.zeros((rows // capacity, PAD - capacity, depth), own.dtype)
    for g, part in enumerate((jnp.where(low, own, other), jnp.where(low, other, own))):
        spaced = jnp.concatenate([part.reshape(rows // capacity, capacity, depth), empty], axis=1)
        out_ref[g] = spaced.reshape(rows // capacity * PAD, depth)


def put_lines(capacity, rows_ref, weights, lines_ref, start, end):
    targets, _, lanes = lines_ref.shape
    products = [
        lax.dot_general(
            rows_ref[...], ref[...], (((1,), (1,)), ((), ())), preferred_element_type=jnp.float32
        )
        for ref in weights
    ]
    width = sum(product.shape[1] for product in products)
    blocks = -(-width // lanes)
    if blocks * lanes > width:
        products.append(jnp.zeros((targets * PAD, blocks * lanes - width), jnp.float32))
    product = jnp.concatenate(products, axis=1).reshape(targets, PAD, blocks * lanes)
    for j in range(blocks):
        lines_ref[:, start + j * capacity : start + (j + 1) * capacity, :] = product[
            :, :capacity, j * lanes : (j + 1) * lanes
        ]
    done = start + blocks * capacity
    if end > done:
        lines_ref[:, done:end, :] = jnp.zeros((targets, end - done, lanes), jnp.float32)


def products_kernel(capacity, rows_ref, *refs):
    weights, (out_ref, lines_ref) = refs[:-2], refs[-2:]
    put_lines(capacity, rows_ref, weights, lines_ref, 0, out_ref.shape[1])
    out_ref[...] = lines_ref[...].astype(out_ref.dtype)


def routed_sums(capacity, combine, chunk_ref, lines_ref):
    targets, lines, lanes = chunk_ref.shape
    blocks = lines // capacity
    lines_ref[:, :lines, :] = chunk_ref[...].astype(jnp.float32)
    lines_ref[:, lines : lines + PAD, :] = jnp.zeros((targets, PAD, lanes), jnp.float32)
    columns = [
        lines_ref[:, j * capacity : j * capacity + PAD, :].reshape(targets * PAD, lanes)
        for j in range(blocks)
    ]
    rows = jnp.concatenate(columns, axis=1).astype(jnp.bfloat16)
    half = combine.shape[1]
    return [
        jnp.dot(combine, rows[g * half : (g + 1) * half], preferred_element_type=jnp.float32)
        for g in range(rows.shape[0] // half)
    ]


def more_products_kernel(capacity, held, rows_ref, begun_ref, *refs):
    weights, (out_ref, lines_ref) = refs[:-2], refs[-2:]
    lines = out_ref.shape[1]
    lines_ref[:, : begun_ref.shape[1], :] = begun_ref[...].astype(jnp.float32)
    put_lines(capacity, rows_ref, weights, lines_ref, held, lines)
    out_ref[...] = lines_ref[...].astype(out_ref.dtype)


def halves_kernel(half, low_ref, high_ref, low_out, high_out, semaphores):
    copies = [
        pltpu.make_async_copy(low_ref.at[:half], low_out, semaphores.at[0]),
        pltpu.make_async_copy(high_ref.at[half:], high_out, semaphores.at[1]),
    ]
    for copy in copies:
        copy.start()
    for copy in copies:
        copy.wait()


def finish_kernel(capacity, layout, z_ref, combine_ref, key_ref, rope_ref, *refs):
    chunks, (out_ref, pieces_ref, lines_ref) = refs[:-3], refs[-3:]
    pairs, ring, tokens, piece = pieces_ref.shape
    z = z_ref[0]
    for chunk, distances in zip(chunks, layout):
        for g, routed in enumerate(routed_sums(capacity, combine_ref[...], chunk, lines_ref)):
            for start, distance in distances:
                pieces_ref[g, distance % ring] = routed[:, start : start + piece]
    for g in range(pairs):
        for h in range(ring // 2):
            left = pieces_ref[g, lax.rem(2 * h - z + ring, ring)]
            right = pieces_ref[g, lax.rem(2 * h + 1 - z + ring, ring)]
            columns = slice((g * ring + 2 * h) * piece, (g * ring + 2 * h + 2) * piece)
            attention = jnp.dot(
                key_ref[...], rope_ref[:, columns], preferred_element_type=jnp.float32
            )
            routed = jnp.concatenate([left, right], axis=1)
            out_ref[:, columns] = (routed + attention).astype(out_ref.dtype)


def body(routes, route_weights, hidden_grads, expert_weight, normed, key_grad, rope_weight):
    groups = lax.axis_size(DP)
    experts_here = lax.axis_size(EXPERT)
    pairs = lax.axis_size("ylo")
    ring = lax.axis_size("z")
    slot_rows = hidden_grads[0]
    projection = expert_weight[0]
    depth = slot_rows.shape[1]
    capacity = slot_rows.shape[0] // experts_here
    piece = projection.shape[0]
    tokens, key_size = key_grad.shape
    width = piece * groups
    share = width // experts_here
    last = ring // 2
    rows = experts_here * PAD
    z = lax.axis_index("z").astype(jnp.int32).reshape(1)
    low = (lax.axis_index("ylo") == 0).astype(jnp.int32).reshape(1)
    up = [(i, (i + 1) % ring) for i in range(ring)]
    down = [(i, (i - 1) % ring) for i in range(ring)]

    packed = key_size * share // 128
    cores = lax.axis_size("core")
    places = tuple(
        tuple(place * cores + core for core in range(cores)) for place in range(experts_here // cores)
    )
    swap = [(0, 1), (1, 0)]
    mine = call(
        functools.partial(partial_kernel, places),
        struct((len(places), packed, 128), jnp.float32),
        [SMEM] + [VMEM] * 4,
        4 * tokens * key_size * width,
        4 * 10**6,
    )(
        lax.axis_index("core").astype(jnp.int32).reshape(1),
        normed,
        key_grad,
        lax.ppermute(normed, "core", swap),
        lax.ppermute(key_grad, "core", swap),
    )
    terms = lax.all_to_all(mine, ("x", "yhi"), split_axis=0, concat_axis=0, tiled=True)
    mine = jnp.sum(terms, axis=0)

    other = lax.ppermute(slot_rows, "ylo", swap)

    def spaced_rows(other):
        return call(
            functools.partial(rows_kernel, capacity),
            struct((pairs, rows, depth), jnp.bfloat16),
            [SMEM, VMEM, VMEM],
            0,
            3 * 10**6,
        )(low, slot_rows, other).reshape(pairs * rows, depth)

    def products(weights, flops, after=()):
        columns = sum(w.shape[0] for w in weights)
        lines = -(-(-(-columns // 128) * capacity) // 16) * 16
        shape = (pairs * experts_here, lines, 128)
        return call(
            functools.partial(products_kernel, capacity),
            struct(shape, jnp.bfloat16),
            [VMEM] * (1 + len(weights)),
            flops,
            4 * 10**6,
            [pltpu.VMEM(shape, jnp.float32)],
            after,
        )(both, *weights)

    def added(sums, bit):
        return sums + lax.ppermute(sums, "z", [(i, i ^ bit) for i in range(ring)])

    def more_products(begun, columns, weights, flops, after=()):
        shape = (pairs * experts_here, 48, 128)
        return call(
            functools.partial(more_products_kernel, capacity, -(-columns // 128) * capacity),
            struct(shape, jnp.bfloat16),
            [VMEM] * (2 + len(weights)),
            flops,
            3 * 10**6,
            [pltpu.VMEM(shape, jnp.float32)],
            after,
        )(both, begun, *weights)

    def send(computed):
        return lax.all_to_all(computed, PLANE, split_axis=0, concat_axis=0, tiled=True)

    whole = -(-piece // 128) * 128
    layout = (
        ((0, 0), (whole, -1), (whole + piece, 1)),
        ((0, -2), (piece, 2)),
        ((0, -3), (piece, 3), (2 * piece, 4)),
    )
    below, above = [projection], [projection]
    below.append(lax.ppermute(below[-1], "z", up))
    above.append(lax.ppermute(above[-1], "z", down))
    both = spaced_rows(other)
    begun = products([projection], 1 * 10**9)
    below[1], above[1], begun = lax.optimization_barrier((below[1], above[1], begun))
    first = more_products(begun, piece, [below[1], above[1]], 2 * 10**9)
    first, mine = lax.optimization_barrier((first, mine))
    below.append(lax.ppermute(below[-1], "z", up))
    above.append(lax.ppermute(above[-1], "z", down))
    below[2], _ = lax.optimization_barrier((below[2], first))
    above[2], _ = lax.optimization_barrier((above[2], first))
    second = products([below[2], above[2]], 15 * 10**9)
    below.append(lax.ppermute(below[-1], "z", up))
    above.append(lax.ppermute(above[-1], "z", down))
    sent = [send(first)]
    half = piece // 2
    half_low, half_high = call(
        functools.partial(halves_kernel, half),
        [struct((half, depth), jnp.bfloat16)] * 2,
        [ANY] * 2,
        0,
        3 * 10**6,
        [pltpu.SemaphoreType.DMA((2,))],
        [second] + sent,
        ANY,
    )(below[-1], above[-1])
    last_low = lax.ppermute(half_low, "z", up)
    last_high = lax.ppermute(half_high, "z", down)
    sent.append(send(second))
    two = added(added(mine, 1), 2)
    begun = products([below[3], above[3]], 10 * 10**9)
    third = more_products(begun, 2 * piece, [last_low, last_high], 1 * 10**9, [two])
    chunks = sent + [send(third)]

    combine = call(
        functools.partial(combine_kernel, experts_here, capacity),
        struct((tokens, rows), jnp.bfloat16),
        [VMEM, VMEM],
        10**7,
        10**6,
    )(routes, route_weights)
    most = max(chunk.shape[1] for chunk in chunks)
    lines = pltpu.VMEM((pairs * experts_here, most + PAD, 128), jnp.float32)
    summed = added(two, 4)
    summed = summed + lax.ppermute(summed, "ylo", swap)
    scale_factor = (tokens * groups * experts_here) ** (-0.5)
    rope_grad = call(
        functools.partial(rope_kernel, key_size, share, scale_factor),
        struct((key_size, share), jnp.float32),
        [VMEM],
        0,
        10**6,
    )(summed)

    token_grad = call(
        functools.partial(finish_kernel, capacity, layout),
        struct((tokens, width), jnp.bfloat16),
        [SMEM] + [VMEM] * (3 + len(chunks)),
        4 * 10**8,
        6 * 10**6,
        [pltpu.VMEM((pairs, ring, tokens, piece), jnp.float32), lines],
    )(z, combine, key_grad, rope_weight, *chunks)
    return (token_grad, rope_grad)


def solution(mesh):
    wide = Mesh(mesh.devices.reshape(2, 8, 4, 4, 2), ALL)
    return jax.shard_map(
        body,
        mesh=wide,
        in_specs=(
            P(ALL, None),
            P(ALL, None),
            P(EXPERT, DP, None),
            P(EXPERT, DP, None),
            P(ALL, None),
            P(ALL, None),
            P(),
        ),
        out_specs=(P(ALL, None), P(None, EXPERT)),
        check_vma=False,
    )
```

```python
import functools

import jax
import jax.numpy as jnp
from jax import lax
from jax.experimental import pallas as pl
from jax.experimental.pallas import tpu as pltpu
from jax.sharding import Mesh
from jax.sharding import PartitionSpec as P

EXP_DEV = 5
PAD = 8

DP = ("ylo", "z")
EXPERT = ("x", "yhi", "core")
ALL = DP + EXPERT
PLANE = ("ylo",) + EXPERT

VMEM = pl.BlockSpec(memory_space=pltpu.VMEM)
SMEM = pl.BlockSpec(memory_space=pltpu.SMEM)
ANY = pl.BlockSpec(memory_space=pl.ANY)


def call(kernel, out_shape, in_specs, flops, moved, scratch=(), after=(), out_spec=VMEM):
    taken = len(in_specs)

    def without(*refs):
        kernel(*refs[:taken], *refs[taken + len(after) :])

    run = pl.pallas_call(
        without,
        out_shape=out_shape,
        in_specs=list(in_specs) + [ANY] * len(after),
        out_specs=jax.tree.map(lambda _: out_spec, out_shape),
        scratch_shapes=list(scratch),
        compiler_params=pltpu.CompilerParams(vmem_limit_bytes=16 * 1024 * 1024),
        cost_estimate=pl.CostEstimate(flops=flops, bytes_accessed=moved, transcendentals=0),
    )
    return lambda *args: run(*args, *after)


def struct(shape, dtype):
    return jax.ShapeDtypeStruct(shape, dtype)


def partial_kernel(places, core_ref, normed_ref, key_ref, other_normed_ref, other_key_ref, out_ref):
    dims = (((1,), (0,)), ((), ()))
    product = lax.dot_general(
        key_ref[...], normed_ref[...], dims, preferred_element_type=jnp.float32
    ) + lax.dot_general(
        other_key_ref[...], other_normed_ref[...], dims, preferred_element_type=jnp.float32
    )
    key, width = product.shape
    share = width // (2 * len(places))
    rest = share - 128
    group = key * rest // 128
    first = core_ref[0] == 0
    for place, (low, high) in enumerate(places):
        part = jnp.where(
            first,
            product[:, low * share : (low + 1) * share],
            product[:, high * share : (high + 1) * share],
        )
        out_ref[place, :key, :] = part[:, :128]
        out_ref[place, key:, :] = jnp.concatenate(
            [part[a * group : (a + 1) * group, 128:] for a in range(key // group)], axis=1
        )


def rope_kernel(key, share, scale_factor, total_ref, out_ref):
    total = total_ref[...] * scale_factor
    rest = share - 128
    tail = jnp.concatenate([total[key:, a * rest : (a + 1) * rest] for a in range(128 // rest)], axis=0)
    out_ref[...] = jnp.concatenate([total[:key, :], tail], axis=1)


def combine_kernel(experts, capacity, routes_ref, weights_ref, out_ref):
    tokens, topk = routes_ref.shape
    expert = lax.broadcasted_iota(jnp.int32, (tokens, experts), 1)
    chosen = jnp.zeros((tokens, experts), jnp.float32)
    weight = jnp.zeros((tokens, experts), jnp.float32)
    for k in range(topk):
        here = routes_ref[:, k : k + 1] == expert * EXP_DEV
        chosen = jnp.where(here, 1.0, chosen)
        weight = jnp.where(here, weights_ref[:, k : k + 1], weight)
    row = lax.broadcasted_iota(jnp.int32, (tokens, tokens), 0)
    column = lax.broadcasted_iota(jnp.int32, (tokens, tokens), 1)
    before = (column < row).astype(jnp.bfloat16)
    slot = jnp.dot(before, chosen.astype(jnp.bfloat16), preferred_element_type=jnp.float32)
    slot = jnp.where(chosen > 0.0, slot, 128.0)
    spread = (
        lax.broadcasted_iota(jnp.int32, (experts, experts * PAD), 1) // PAD
        == lax.broadcasted_iota(jnp.int32, (experts, experts * PAD), 0)
    ).astype(jnp.bfloat16)
    slots = jnp.dot(slot.astype(jnp.bfloat16), spread, preferred_element_type=jnp.float32)
    weights = jnp.dot(weight.astype(jnp.bfloat16), spread, preferred_element_type=jnp.float32)
    place = lax.rem(lax.broadcasted_iota(jnp.int32, slots.shape, 1), PAD)
    kept = (slots == place.astype(jnp.float32)) & (place < capacity)
    out_ref[...] = jnp.where(kept, weights, 0.0).astype(out_ref.dtype)


def rows_kernel(capacity, low_ref, own_ref, other_ref, out_ref):
    own, other = own_ref[...], other_ref[...]
    low = low_ref[0] == 1
    rows, depth = own.shape
    empty = jnp.zeros((rows // capacity, PAD - capacity, depth), own.dtype)
    for g, part in enumerate((jnp.where(low, own, other), jnp.where(low, other, own))):
        spaced = jnp.concatenate([part.reshape(rows // capacity, capacity, depth), empty], axis=1)
        out_ref[g] = spaced.reshape(rows // capacity * PAD, depth)


def put_lines(capacity, rows_ref, weights, lines_ref, start, end):
    targets, _, lanes = lines_ref.shape
    products = [
        lax.dot_general(
            rows_ref[...], ref[...], (((1,), (1,)), ((), ())), preferred_element_type=jnp.float32
        )
        for ref in weights
    ]
    width = sum(product.shape[1] for product in products)
    blocks = -(-width // lanes)
    if blocks * lanes > width:
        products.append(jnp.zeros((targets * PAD, blocks * lanes - width), jnp.float32))
    product = jnp.concatenate(products, axis=1).reshape(targets, PAD, blocks * lanes)
    for j in range(blocks):
        lines_ref[:, start + j * capacity : start + (j + 1) * capacity, :] = product[
            :, :capacity, j * lanes : (j + 1) * lanes
        ]
    done = start + blocks * capacity
    if end > done:
        lines_ref[:, done:end, :] = jnp.zeros((targets, end - done, lanes), jnp.float32)


def products_kernel(capacity, rows_ref, *refs):
    weights, (out_ref, lines_ref) = refs[:-2], refs[-2:]
    put_lines(capacity, rows_ref, weights, lines_ref, 0, out_ref.shape[1])
    out_ref[...] = lines_ref[...].astype(out_ref.dtype)


def routed_sums(capacity, combine, chunk_ref, lines_ref):
    targets, lines, lanes = chunk_ref.shape
    blocks = lines // capacity
    lines_ref[:, :lines, :] = chunk_ref[...].astype(jnp.float32)
    lines_ref[:, lines : lines + PAD, :] = jnp.zeros((targets, PAD, lanes), jnp.float32)
    columns = [
        lines_ref[:, j * capacity : j * capacity + PAD, :].reshape(targets * PAD, lanes)
        for j in range(blocks)
    ]
    rows = jnp.concatenate(columns, axis=1).astype(jnp.bfloat16)
    half = combine.shape[1]
    return [
        jnp.dot(combine, rows[g * half : (g + 1) * half], preferred_element_type=jnp.float32)
        for g in range(rows.shape[0] // half)
    ]


def more_products_kernel(capacity, held, rows_ref, begun_ref, *refs):
    weights, (out_ref, lines_ref) = refs[:-2], refs[-2:]
    lines = out_ref.shape[1]
    lines_ref[:, : begun_ref.shape[1], :] = begun_ref[...].astype(jnp.float32)
    put_lines(capacity, rows_ref, weights, lines_ref, held, lines)
    out_ref[...] = lines_ref[...].astype(out_ref.dtype)


def halves_kernel(half, low_ref, high_ref, low_out, high_out, semaphores):
    copies = [
        pltpu.make_async_copy(low_ref.at[:half], low_out, semaphores.at[0]),
        pltpu.make_async_copy(high_ref.at[half:], high_out, semaphores.at[1]),
    ]
    for copy in copies:
        copy.start()
    for copy in copies:
        copy.wait()


def finish_kernel(capacity, layout, z_ref, combine_ref, key_ref, rope_ref, *refs):
    chunks, (out_ref, pieces_ref, lines_ref) = refs[:-3], refs[-3:]
    pairs, ring, tokens, piece = pieces_ref.shape
    z = z_ref[0]
    side = 1 - 2 * lax.rem(z, 2)
    for chunk, distances in zip(chunks, layout):
        for g, routed in enumerate(routed_sums(capacity, combine_ref[...], chunk, lines_ref)):
            for start, distance in distances:
                there = lax.rem(distance * side + ring, ring)
                pieces_ref[g, there] = routed[:, start : start + piece]
    for g in range(pairs):
        for h in range(ring // 2):
            left = pieces_ref[g, lax.rem(2 * h - z + ring, ring)]
            right = pieces_ref[g, lax.rem(2 * h + 1 - z + ring, ring)]
            columns = slice((g * ring + 2 * h) * piece, (g * ring + 2 * h + 2) * piece)
            attention = lax.dot_general(
                key_ref[...],
                rope_ref[:, columns],
                (((0,), (0,)), ((), ())),
                preferred_element_type=jnp.float32,
            )
            routed = jnp.concatenate([left, right], axis=1)
            out_ref[:, columns] = (routed + attention).astype(out_ref.dtype)


def body(routes, route_weights, hidden_grads, expert_weight, normed, key_grad, rope_weight):
    groups = lax.axis_size(DP)
    experts_here = lax.axis_size(EXPERT)
    pairs = lax.axis_size("ylo")
    ring = lax.axis_size("z")
    slot_rows = hidden_grads[0]
    projection = expert_weight[0]
    depth = slot_rows.shape[1]
    capacity = slot_rows.shape[0] // experts_here
    piece = projection.shape[0]
    tokens, key_size = key_grad.shape
    key_lines = key_grad.T
    width = piece * groups
    share = width // experts_here
    last = ring // 2
    rows = experts_here * PAD
    z = lax.axis_index("z").astype(jnp.int32).reshape(1)
    low = (lax.axis_index("ylo") == 0).astype(jnp.int32).reshape(1)
    inner = [(i, (i + 1 - 2 * (i % 2)) % ring) for i in range(ring)]
    outer = [(i, (i - 1 + 2 * (i % 2)) % ring) for i in range(ring)]

    packed = key_size * share // 128
    cores = lax.axis_size("core")
    places = tuple(
        tuple(place * cores + core for core in range(cores)) for place in range(experts_here // cores)
    )
    swap = [(0, 1), (1, 0)]
    mine = call(
        functools.partial(partial_kernel, places),
        struct((len(places), packed, 128), jnp.float32),
        [SMEM] + [VMEM] * 4,
        4 * tokens * key_size * width,
        4 * 10**6,
    )(
        lax.axis_index("core").astype(jnp.int32).reshape(1),
        normed,
        key_lines,
        lax.ppermute(normed, "core", swap),
        lax.ppermute(key_lines, "core", swap),
    )
    terms = lax.all_to_all(mine, ("x", "yhi"), split_axis=0, concat_axis=0, tiled=True)

    other = lax.ppermute(slot_rows, "ylo", swap)

    def spaced_rows(other):
        return call(
            functools.partial(rows_kernel, capacity),
            struct((pairs, rows, depth), jnp.bfloat16),
            [SMEM, VMEM, VMEM],
            0,
            3 * 10**6,
        )(low, slot_rows, other).reshape(pairs * rows, depth)

    def products(weights, flops, after=()):
        columns = sum(w.shape[0] for w in weights)
        lines = -(-(-(-columns // 128) * capacity) // 16) * 16
        shape = (pairs * experts_here, lines, 128)
        return call(
            functools.partial(products_kernel, capacity),
            struct(shape, jnp.bfloat16),
            [VMEM] * (1 + len(weights)),
            flops,
            4 * 10**6,
            [pltpu.VMEM(shape, jnp.float32)],
            after,
        )(both, *weights)

    def added(sums, bit):
        return sums + lax.ppermute(sums, "z", [(i, i ^ bit) for i in range(ring)])

    def more_products(begun, columns, weights, flops, after=()):
        shape = (pairs * experts_here, 48, 128)
        return call(
            functools.partial(more_products_kernel, capacity, -(-columns // 128) * capacity),
            struct(shape, jnp.bfloat16),
            [VMEM] * (2 + len(weights)),
            flops,
            3 * 10**6,
            [pltpu.VMEM(shape, jnp.float32)],
            after,
        )(both, begun, *weights)

    def send(computed):
        return lax.all_to_all(computed, PLANE, split_axis=0, concat_axis=0, tiled=True)

    whole = -(-piece // 128) * 128
    layout = (
        ((0, 0), (whole, -1), (whole + piece, 1)),
        ((0, -2), (piece, 2)),
        ((0, -3), (piece, 3), (2 * piece, 4)),
    )
    paired, crossed = [projection], [projection]
    came = lax.ppermute(crossed[-1], "z", inner), lax.ppermute(paired[-1], "z", outer)
    paired.append(came[0])
    crossed.append(came[1])
    both = spaced_rows(other)
    begun = products([projection], 1 * 10**9)
    crossed[1], paired[1], begun = lax.optimization_barrier((crossed[1], paired[1], begun))
    first = more_products(begun, piece, [crossed[1], paired[1]], 2 * 10**9)
    first, terms = lax.optimization_barrier((first, terms))
    mine = jnp.sum(terms, axis=0)
    came = lax.ppermute(crossed[-1], "z", inner), lax.ppermute(paired[-1], "z", outer)
    paired.append(came[0])
    crossed.append(came[1])
    crossed[2], _ = lax.optimization_barrier((crossed[2], first))
    paired[2], _ = lax.optimization_barrier((paired[2], first))
    second = products([crossed[2], paired[2]], 15 * 10**9)
    came = lax.ppermute(crossed[-1], "z", inner), lax.ppermute(paired[-1], "z", outer)
    paired.append(came[0])
    crossed.append(came[1])
    sent = [send(first)]
    half = piece // 2
    half_low, half_high = call(
        functools.partial(halves_kernel, half),
        [struct((half, depth), jnp.bfloat16)] * 2,
        [ANY] * 2,
        0,
        3 * 10**6,
        [pltpu.SemaphoreType.DMA((2,))],
        [second] + sent,
        ANY,
    )(crossed[-1], paired[-1])
    last_low = lax.ppermute(half_low, "z", inner)
    last_high = lax.ppermute(half_high, "z", outer)
    sent.append(send(second))
    two = added(added(mine, 1), 2)
    begun = products([crossed[3], paired[3]], 10 * 10**9)
    third = more_products(begun, 2 * piece, [last_low, last_high], 1 * 10**9, [two])
    chunks = sent + [send(third)]

    combine = call(
        functools.partial(combine_kernel, experts_here, capacity),
        struct((tokens, rows), jnp.bfloat16),
        [VMEM, VMEM],
        10**7,
        10**6,
    )(routes, route_weights)
    most = max(chunk.shape[1] for chunk in chunks)
    lines = pltpu.VMEM((pairs * experts_here, most + PAD, 128), jnp.float32)
    summed = added(two, 4)
    summed = summed + lax.ppermute(summed, "ylo", swap)
    scale_factor = (tokens * groups * experts_here) ** (-0.5)
    rope_grad = call(
        functools.partial(rope_kernel, key_size, share, scale_factor),
        struct((key_size, share), jnp.float32),
        [VMEM],
        0,
        10**6,
    )(summed)

    token_grad = call(
        functools.partial(finish_kernel, capacity, layout),
        struct((tokens, width), jnp.bfloat16),
        [SMEM] + [VMEM] * (3 + len(chunks)),
        4 * 10**8,
        6 * 10**6,
        [pltpu.VMEM((pairs, ring, tokens, piece), jnp.float32), lines],
    )(z, combine, key_lines, rope_weight, *chunks)
    return (token_grad, rope_grad)


def solution(mesh):
    wide = Mesh(mesh.devices.reshape(2, 8, 4, 4, 2), ALL)
    return jax.shard_map(
        body,
        mesh=wide,
        in_specs=(
            P(ALL, None),
            P(ALL, None),
            P(EXPERT, DP, None),
            P(EXPERT, DP, None),
            P(ALL, None),
            P(ALL, None),
            P(),
        ),
        out_specs=(P(ALL, None), P(None, EXPERT)),
        check_vma=False,
    )
```

```python
import functools

import jax
import jax.numpy as jnp
from jax import lax
from jax.experimental import pallas as pl
from jax.experimental.pallas import tpu as pltpu
from jax.sharding import Mesh
from jax.sharding import PartitionSpec as P

EXP_DEV = 5
PAD = 8

DP = ("ylo", "z")
EXPERT = ("x", "yhi", "core")
ALL = DP + EXPERT
PLANE = ("ylo",) + EXPERT

VMEM = pl.BlockSpec(memory_space=pltpu.VMEM)
SMEM = pl.BlockSpec(memory_space=pltpu.SMEM)
ANY = pl.BlockSpec(memory_space=pl.ANY)


def call(kernel, out_shape, in_specs, flops, moved, scratch=(), after=(), out_spec=VMEM):
    taken = len(in_specs)

    def without(*refs):
        kernel(*refs[:taken], *refs[taken + len(after) :])

    run = pl.pallas_call(
        without,
        out_shape=out_shape,
        in_specs=list(in_specs) + [ANY] * len(after),
        out_specs=jax.tree.map(lambda _: out_spec, out_shape),
        scratch_shapes=list(scratch),
        compiler_params=pltpu.CompilerParams(vmem_limit_bytes=16 * 1024 * 1024),
        cost_estimate=pl.CostEstimate(flops=flops, bytes_accessed=moved, transcendentals=0),
    )
    return lambda *args: run(*args, *after)


def struct(shape, dtype):
    return jax.ShapeDtypeStruct(shape, dtype)


def partial_kernel(places, core_ref, normed_ref, key_ref, other_normed_ref, other_key_ref, out_ref):
    dims = (((1,), (0,)), ((), ()))
    product = lax.dot_general(
        key_ref[...], normed_ref[...], dims, preferred_element_type=jnp.float32
    ) + lax.dot_general(
        other_key_ref[...], other_normed_ref[...], dims, preferred_element_type=jnp.float32
    )
    key, width = product.shape
    share = width // (2 * len(places))
    rest = share - 128
    group = key * rest // 128
    first = core_ref[0] == 0
    for place, (low, high) in enumerate(places):
        part = jnp.where(
            first,
            product[:, low * share : (low + 1) * share],
            product[:, high * share : (high + 1) * share],
        )
        out_ref[place, :key, :] = part[:, :128]
        out_ref[place, key:, :] = jnp.concatenate(
            [part[a * group : (a + 1) * group, 128:] for a in range(key // group)], axis=1
        )


def rope_kernel(key, share, scale_factor, total_ref, out_ref):
    total = total_ref[...] * scale_factor
    rest = share - 128
    tail = jnp.concatenate([total[key:, a * rest : (a + 1) * rest] for a in range(128 // rest)], axis=0)
    out_ref[...] = jnp.concatenate([total[:key, :], tail], axis=1)


def combine_kernel(experts, capacity, routes_ref, weights_ref, out_ref):
    tokens, topk = routes_ref.shape
    expert = lax.broadcasted_iota(jnp.int32, (tokens, experts), 1)
    chosen = jnp.zeros((tokens, experts), jnp.float32)
    weight = jnp.zeros((tokens, experts), jnp.float32)
    for k in range(topk):
        here = routes_ref[:, k : k + 1] == expert * EXP_DEV
        chosen = jnp.where(here, 1.0, chosen)
        weight = jnp.where(here, weights_ref[:, k : k + 1], weight)
    row = lax.broadcasted_iota(jnp.int32, (tokens, tokens), 0)
    column = lax.broadcasted_iota(jnp.int32, (tokens, tokens), 1)
    before = (column < row).astype(jnp.bfloat16)
    slot = jnp.dot(before, chosen.astype(jnp.bfloat16), preferred_element_type=jnp.float32)
    slot = jnp.where(chosen > 0.0, slot, 128.0)
    spread = (
        lax.broadcasted_iota(jnp.int32, (experts, experts * PAD), 1) // PAD
        == lax.broadcasted_iota(jnp.int32, (experts, experts * PAD), 0)
    ).astype(jnp.bfloat16)
    slots = jnp.dot(slot.astype(jnp.bfloat16), spread, preferred_element_type=jnp.float32)
    weights = jnp.dot(weight.astype(jnp.bfloat16), spread, preferred_element_type=jnp.float32)
    place = lax.rem(lax.broadcasted_iota(jnp.int32, slots.shape, 1), PAD)
    kept = (slots == place.astype(jnp.float32)) & (place < capacity)
    out_ref[...] = jnp.where(kept, weights, 0.0).astype(out_ref.dtype)


def rows_kernel(capacity, low_ref, own_ref, other_ref, out_ref):
    own, other = own_ref[...], other_ref[...]
    low = low_ref[0] == 1
    rows, depth = own.shape
    empty = jnp.zeros((rows // capacity, PAD - capacity, depth), own.dtype)
    for g, part in enumerate((jnp.where(low, own, other), jnp.where(low, other, own))):
        spaced = jnp.concatenate([part.reshape(rows // capacity, capacity, depth), empty], axis=1)
        out_ref[g] = spaced.reshape(rows // capacity * PAD, depth)


def put_lines(capacity, rows_ref, weights, lines_ref, start, end):
    targets, _, lanes = lines_ref.shape
    products = [
        lax.dot_general(
            rows_ref[...], ref[...], (((1,), (1,)), ((), ())), preferred_element_type=jnp.float32
        )
        for ref in weights
    ]
    width = sum(product.shape[1] for product in products)
    blocks = -(-width // lanes)
    if blocks * lanes > width:
        products.append(jnp.zeros((targets * PAD, blocks * lanes - width), jnp.float32))
    product = jnp.concatenate(products, axis=1).reshape(targets, PAD, blocks * lanes)
    for j in range(blocks):
        lines_ref[:, start + j * capacity : start + (j + 1) * capacity, :] = product[
            :, :capacity, j * lanes : (j + 1) * lanes
        ]
    done = start + blocks * capacity
    if end > done:
        lines_ref[:, done:end, :] = jnp.zeros((targets, end - done, lanes), jnp.float32)


def products_kernel(capacity, rows_ref, *refs):
    weights, (out_ref, lines_ref) = refs[:-2], refs[-2:]
    put_lines(capacity, rows_ref, weights, lines_ref, 0, out_ref.shape[1])
    out_ref[...] = lines_ref[...].astype(out_ref.dtype)


def routed_sums(capacity, combine, chunk_ref, lines_ref):
    targets, lines, lanes = chunk_ref.shape
    blocks = lines // capacity
    lines_ref[:, :lines, :] = chunk_ref[...].astype(jnp.float32)
    lines_ref[:, lines : lines + PAD, :] = jnp.zeros((targets, PAD, lanes), jnp.float32)
    columns = [
        lines_ref[:, j * capacity : j * capacity + PAD, :].reshape(targets * PAD, lanes)
        for j in range(blocks)
    ]
    rows = jnp.concatenate(columns, axis=1).astype(jnp.bfloat16)
    half = combine.shape[1]
    return [
        jnp.dot(combine, rows[g * half : (g + 1) * half], preferred_element_type=jnp.float32)
        for g in range(rows.shape[0] // half)
    ]


def more_products_kernel(capacity, held, rows_ref, begun_ref, *refs):
    weights, (out_ref, lines_ref) = refs[:-2], refs[-2:]
    lines = out_ref.shape[1]
    lines_ref[:, : begun_ref.shape[1], :] = begun_ref[...].astype(jnp.float32)
    put_lines(capacity, rows_ref, weights, lines_ref, held, lines)
    out_ref[...] = lines_ref[...].astype(out_ref.dtype)


def halves_kernel(half, low_ref, high_ref, low_out, high_out, semaphores):
    copies = [
        pltpu.make_async_copy(low_ref.at[:half], low_out, semaphores.at[0]),
        pltpu.make_async_copy(high_ref.at[half:], high_out, semaphores.at[1]),
    ]
    for copy in copies:
        copy.start()
    for copy in copies:
        copy.wait()


def finish_kernel(capacity, layout, z_ref, combine_ref, key_ref, rope_ref, *refs):
    chunks, (out_ref, pieces_ref, lines_ref, ready_ref, semaphores) = refs[:-5], refs[-5:]
    pairs, ring, tokens, piece = pieces_ref.shape
    z = z_ref[0]
    side = 1 - 2 * lax.rem(z, 2)
    for chunk, distances in zip(chunks, layout):
        for g, routed in enumerate(routed_sums(capacity, combine_ref[...], chunk, lines_ref)):
            for start, distance in distances:
                there = lax.rem(distance * side + ring, ring)
                pieces_ref[g, there] = routed[:, start : start + piece]
    copies = []
    for g in range(pairs):
        for h in range(ring // 2):
            left = pieces_ref[g, lax.rem(2 * h - z + ring, ring)]
            right = pieces_ref[g, lax.rem(2 * h + 1 - z + ring, ring)]
            columns = slice((g * ring + 2 * h) * piece, (g * ring + 2 * h + 2) * piece)
            attention = lax.dot_general(
                key_ref[...],
                rope_ref[:, columns],
                (((0,), (0,)), ((), ())),
                preferred_element_type=jnp.float32,
            )
            routed = jnp.concatenate([left, right], axis=1)
            ready_ref[:, columns] = (routed + attention).astype(ready_ref.dtype)
            copy = pltpu.make_async_copy(
                ready_ref.at[:, columns], out_ref.at[:, columns], semaphores.at[len(copies)]
            )
            copy.start()
            copies.append(copy)
    for copy in copies:
        copy.wait()


def body(routes, route_weights, hidden_grads, expert_weight, normed, key_grad, rope_weight):
    groups = lax.axis_size(DP)
    experts_here = lax.axis_size(EXPERT)
    pairs = lax.axis_size("ylo")
    ring = lax.axis_size("z")
    slot_rows = hidden_grads[0]
    projection = expert_weight[0]
    depth = slot_rows.shape[1]
    capacity = slot_rows.shape[0] // experts_here
    piece = projection.shape[0]
    tokens, key_size = key_grad.shape
    key_lines = key_grad.T
    width = piece * groups
    share = width // experts_here
    last = ring // 2
    rows = experts_here * PAD
    z = lax.axis_index("z").astype(jnp.int32).reshape(1)
    low = (lax.axis_index("ylo") == 0).astype(jnp.int32).reshape(1)
    inner = [(i, (i + 1 - 2 * (i % 2)) % ring) for i in range(ring)]
    outer = [(i, (i - 1 + 2 * (i % 2)) % ring) for i in range(ring)]

    packed = key_size * share // 128
    cores = lax.axis_size("core")
    places = tuple(
        tuple(place * cores + core for core in range(cores)) for place in range(experts_here // cores)
    )
    swap = [(0, 1), (1, 0)]
    mine = call(
        functools.partial(partial_kernel, places),
        struct((len(places), packed, 128), jnp.float32),
        [SMEM] + [VMEM] * 4,
        4 * tokens * key_size * width,
        4 * 10**6,
    )(
        lax.axis_index("core").astype(jnp.int32).reshape(1),
        normed,
        key_lines,
        lax.ppermute(normed, "core", swap),
        lax.ppermute(key_lines, "core", swap),
    )
    terms = lax.all_to_all(mine, ("x", "yhi"), split_axis=0, concat_axis=0, tiled=True)

    other = lax.ppermute(slot_rows, "ylo", swap)

    def spaced_rows(other):
        return call(
            functools.partial(rows_kernel, capacity),
            struct((pairs, rows, depth), jnp.bfloat16),
            [SMEM, VMEM, VMEM],
            0,
            3 * 10**6,
        )(low, slot_rows, other).reshape(pairs * rows, depth)

    def products(weights, flops, after=()):
        columns = sum(w.shape[0] for w in weights)
        lines = -(-(-(-columns // 128) * capacity) // 16) * 16
        shape = (pairs * experts_here, lines, 128)
        return call(
            functools.partial(products_kernel, capacity),
            struct(shape, jnp.bfloat16),
            [VMEM] * (1 + len(weights)),
            flops,
            4 * 10**6,
            [pltpu.VMEM(shape, jnp.float32)],
            after,
        )(both, *weights)

    def added(sums, bit):
        return sums + lax.ppermute(sums, "z", [(i, i ^ bit) for i in range(ring)])

    def more_products(begun, columns, weights, flops, after=()):
        shape = (pairs * experts_here, 48, 128)
        return call(
            functools.partial(more_products_kernel, capacity, -(-columns // 128) * capacity),
            struct(shape, jnp.bfloat16),
            [VMEM] * (2 + len(weights)),
            flops,
            3 * 10**6,
            [pltpu.VMEM(shape, jnp.float32)],
            after,
        )(both, begun, *weights)

    def send(computed):
        return lax.all_to_all(computed, PLANE, split_axis=0, concat_axis=0, tiled=True)

    whole = -(-piece // 128) * 128
    layout = (
        ((0, 0), (whole, -1), (whole + piece, 1)),
        ((0, -2), (piece, 2)),
        ((0, -3), (piece, 3), (2 * piece, 4)),
    )
    paired, crossed = [projection], [projection]
    came = lax.ppermute(crossed[-1], "z", inner), lax.ppermute(paired[-1], "z", outer)
    paired.append(came[0])
    crossed.append(came[1])
    both = spaced_rows(other)
    begun = products([projection], 1 * 10**9)
    crossed[1], paired[1], begun = lax.optimization_barrier((crossed[1], paired[1], begun))
    first = more_products(begun, piece, [crossed[1], paired[1]], 2 * 10**9)
    first, terms = lax.optimization_barrier((first, terms))
    mine = jnp.sum(terms, axis=0)
    came = lax.ppermute(crossed[-1], "z", inner), lax.ppermute(paired[-1], "z", outer)
    paired.append(came[0])
    crossed.append(came[1])
    crossed[2], _ = lax.optimization_barrier((crossed[2], first))
    paired[2], _ = lax.optimization_barrier((paired[2], first))
    second = products([crossed[2], paired[2]], 15 * 10**9)
    came = lax.ppermute(crossed[-1], "z", inner), lax.ppermute(paired[-1], "z", outer)
    paired.append(came[0])
    crossed.append(came[1])
    sent = [send(first)]
    half = piece // 2
    half_low, half_high = call(
        functools.partial(halves_kernel, half),
        [struct((half, depth), jnp.bfloat16)] * 2,
        [ANY] * 2,
        0,
        3 * 10**6,
        [pltpu.SemaphoreType.DMA((2,))],
        [second] + sent,
        ANY,
    )(crossed[-1], paired[-1])
    last_low = lax.ppermute(half_low, "z", inner)
    last_high = lax.ppermute(half_high, "z", outer)
    sent.append(send(second))
    two = added(added(mine, 1), 2)
    begun = products([crossed[3], paired[3]], 10 * 10**9)
    third = more_products(begun, 2 * piece, [last_low, last_high], 1 * 10**9, [two])
    chunks = sent + [send(third)]

    combine = call(
        functools.partial(combine_kernel, experts_here, capacity),
        struct((tokens, rows), jnp.bfloat16),
        [VMEM, VMEM],
        10**7,
        10**6,
    )(routes, route_weights)
    most = max(chunk.shape[1] for chunk in chunks)
    lines = pltpu.VMEM((pairs * experts_here, most + PAD, 128), jnp.float32)
    summed = added(two, 4)
    summed = summed + lax.ppermute(summed, "ylo", swap)
    scale_factor = (tokens * groups * experts_here) ** (-0.5)
    rope_grad = call(
        functools.partial(rope_kernel, key_size, share, scale_factor),
        struct((key_size, share), jnp.float32),
        [VMEM],
        0,
        10**6,
    )(summed)

    token_grad = call(
        functools.partial(finish_kernel, capacity, layout),
        struct((tokens, width), jnp.bfloat16),
        [SMEM] + [VMEM] * (3 + len(chunks)),
        4 * 10**8,
        6 * 10**6,
        [
            pltpu.VMEM((pairs, ring, tokens, piece), jnp.float32),
            lines,
            pltpu.VMEM((tokens, width), jnp.bfloat16),
            pltpu.SemaphoreType.DMA((pairs * ring // 2,)),
        ],
        (),
        ANY,
    )(z, combine, key_lines, rope_weight, *chunks)
    return (token_grad, rope_grad)


def solution(mesh):
    wide = Mesh(mesh.devices.reshape(2, 8, 4, 4, 2), ALL)
    return jax.shard_map(
        body,
        mesh=wide,
        in_specs=(
            P(ALL, None),
            P(ALL, None),
            P(EXPERT, DP, None),
            P(EXPERT, DP, None),
            P(ALL, None),
            P(ALL, None),
            P(),
        ),
        out_specs=(P(ALL, None), P(None, EXPERT)),
        check_vma=False,
    )
```

```python
import functools

import jax
import jax.numpy as jnp
from jax import lax
from jax.experimental import pallas as pl
from jax.experimental.pallas import tpu as pltpu
from jax.sharding import Mesh
from jax.sharding import PartitionSpec as P

EXP_DEV = 5
PAD = 8

DP = ("ylo", "z")
EXPERT = ("x", "yhi", "core")
ALL = DP + EXPERT
PLANE = ("ylo",) + EXPERT

VMEM = pl.BlockSpec(memory_space=pltpu.VMEM)
SMEM = pl.BlockSpec(memory_space=pltpu.SMEM)
ANY = pl.BlockSpec(memory_space=pl.ANY)


def call(kernel, out_shape, in_specs, flops, moved, scratch=(), after=(), out_spec=VMEM):
    taken = len(in_specs)

    def without(*refs):
        kernel(*refs[:taken], *refs[taken + len(after) :])

    run = pl.pallas_call(
        without,
        out_shape=out_shape,
        in_specs=list(in_specs) + [ANY] * len(after),
        out_specs=jax.tree.map(lambda _: out_spec, out_shape),
        scratch_shapes=list(scratch),
        compiler_params=pltpu.CompilerParams(vmem_limit_bytes=16 * 1024 * 1024),
        cost_estimate=pl.CostEstimate(flops=flops, bytes_accessed=moved, transcendentals=0),
    )
    return lambda *args: run(*args, *after)


def struct(shape, dtype):
    return jax.ShapeDtypeStruct(shape, dtype)


def partial_kernel(places, core_ref, normed_ref, key_ref, other_normed_ref, other_key_ref, out_ref):
    dims = (((1,), (0,)), ((), ()))
    product = lax.dot_general(
        key_ref[...], normed_ref[...], dims, preferred_element_type=jnp.float32
    ) + lax.dot_general(
        other_key_ref[...], other_normed_ref[...], dims, preferred_element_type=jnp.float32
    )
    key, width = product.shape
    share = width // (2 * len(places))
    rest = share - 128
    group = key * rest // 128
    first = core_ref[0] == 0
    for place, (low, high) in enumerate(places):
        part = jnp.where(
            first,
            product[:, low * share : (low + 1) * share],
            product[:, high * share : (high + 1) * share],
        )
        out_ref[place, :key, :] = part[:, :128]
        out_ref[place, key:, :] = jnp.concatenate(
            [part[a * group : (a + 1) * group, 128:] for a in range(key // group)], axis=1
        )


def rope_kernel(key, share, scale_factor, total_ref, out_ref):
    total = total_ref[...] * scale_factor
    rest = share - 128
    tail = jnp.concatenate([total[key:, a * rest : (a + 1) * rest] for a in range(128 // rest)], axis=0)
    out_ref[...] = jnp.concatenate([total[:key, :], tail], axis=1)


def combine_kernel(experts, capacity, routes_ref, weights_ref, out_ref):
    tokens, topk = routes_ref.shape
    expert = lax.broadcasted_iota(jnp.int32, (tokens, experts), 1)
    chosen = jnp.zeros((tokens, experts), jnp.float32)
    weight = jnp.zeros((tokens, experts), jnp.float32)
    for k in range(topk):
        here = routes_ref[:, k : k + 1] == expert * EXP_DEV
        chosen = jnp.where(here, 1.0, chosen)
        weight = jnp.where(here, weights_ref[:, k : k + 1], weight)
    row = lax.broadcasted_iota(jnp.int32, (tokens, tokens), 0)
    column = lax.broadcasted_iota(jnp.int32, (tokens, tokens), 1)
    before = (column < row).astype(jnp.bfloat16)
    slot = jnp.dot(before, chosen.astype(jnp.bfloat16), preferred_element_type=jnp.float32)
    slot = jnp.where(chosen > 0.0, slot, 128.0)
    spread = (
        lax.broadcasted_iota(jnp.int32, (experts, experts * PAD), 1) // PAD
        == lax.broadcasted_iota(jnp.int32, (experts, experts * PAD), 0)
    ).astype(jnp.bfloat16)
    slots = jnp.dot(slot.astype(jnp.bfloat16), spread, preferred_element_type=jnp.float32)
    weights = jnp.dot(weight.astype(jnp.bfloat16), spread, preferred_element_type=jnp.float32)
    place = lax.rem(lax.broadcasted_iota(jnp.int32, slots.shape, 1), PAD)
    kept = (slots == place.astype(jnp.float32)) & (place < capacity)
    out_ref[...] = jnp.where(kept, weights, 0.0).astype(out_ref.dtype)


def rows_kernel(capacity, low_ref, own_ref, other_ref, out_ref):
    own, other = own_ref[...], other_ref[...]
    low = low_ref[0] == 1
    rows, depth = own.shape
    empty = jnp.zeros((rows // capacity, PAD - capacity, depth), own.dtype)
    for g, part in enumerate((jnp.where(low, own, other), jnp.where(low, other, own))):
        spaced = jnp.concatenate([part.reshape(rows // capacity, capacity, depth), empty], axis=1)
        out_ref[g] = spaced.reshape(rows // capacity * PAD, depth)


def put_lines(capacity, rows_ref, weights, lines_ref, start, end):
    targets, _, lanes = lines_ref.shape
    products = [
        lax.dot_general(
            rows_ref[...], ref[...], (((1,), (1,)), ((), ())), preferred_element_type=jnp.float32
        )
        for ref in weights
    ]
    width = sum(product.shape[1] for product in products)
    blocks = -(-width // lanes)
    if blocks * lanes > width:
        products.append(jnp.zeros((targets * PAD, blocks * lanes - width), jnp.float32))
    product = jnp.concatenate(products, axis=1).reshape(targets, PAD, blocks * lanes)
    for j in range(blocks):
        lines_ref[:, start + j * capacity : start + (j + 1) * capacity, :] = product[
            :, :capacity, j * lanes : (j + 1) * lanes
        ]
    done = start + blocks * capacity
    if end > done:
        lines_ref[:, done:end, :] = jnp.zeros((targets, end - done, lanes), jnp.float32)


def products_kernel(capacity, rows_ref, *refs):
    weights, (out_ref, lines_ref) = refs[:-2], refs[-2:]
    put_lines(capacity, rows_ref, weights, lines_ref, 0, out_ref.shape[1])
    out_ref[...] = lines_ref[...].astype(out_ref.dtype)


def routed_sums(capacity, combine, chunk_ref, lines_ref):
    targets, lines, lanes = chunk_ref.shape
    blocks = lines // capacity
    lines_ref[:, :lines, :] = chunk_ref[...].astype(jnp.float32)
    lines_ref[:, lines : lines + PAD, :] = jnp.zeros((targets, PAD, lanes), jnp.float32)
    columns = [
        lines_ref[:, j * capacity : j * capacity + PAD, :].reshape(targets * PAD, lanes)
        for j in range(blocks)
    ]
    rows = jnp.concatenate(columns, axis=1).astype(jnp.bfloat16)
    half = combine.shape[1]
    return [
        jnp.dot(combine, rows[g * half : (g + 1) * half], preferred_element_type=jnp.float32)
        for g in range(rows.shape[0] // half)
    ]


def more_products_kernel(capacity, held, rows_ref, begun_ref, *refs):
    weights, (out_ref, lines_ref) = refs[:-2], refs[-2:]
    lines = out_ref.shape[1]
    lines_ref[:, : begun_ref.shape[1], :] = begun_ref[...].astype(jnp.float32)
    put_lines(capacity, rows_ref, weights, lines_ref, held, lines)
    out_ref[...] = lines_ref[...].astype(out_ref.dtype)


def cut_kernel(start, rows_ref, out_ref, semaphore):
    copy = pltpu.make_async_copy(rows_ref.at[start : start + out_ref.shape[0]], out_ref, semaphore)
    copy.start()
    copy.wait()


def finish_kernel(capacity, layout, z_ref, combine_ref, key_ref, rope_ref, *refs):
    chunks, (out_ref, pieces_ref, lines_ref, ready_ref, semaphores) = refs[:-5], refs[-5:]
    pairs, ring, tokens, piece = pieces_ref.shape
    z = z_ref[0]
    side = 1 - 2 * lax.rem(z, 2)
    for chunk, distances in zip(chunks, layout):
        for g, routed in enumerate(routed_sums(capacity, combine_ref[...], chunk, lines_ref)):
            for start, distance in distances:
                there = lax.rem(distance * side + ring, ring)
                pieces_ref[g, there] = routed[:, start : start + piece]
    copies = []
    for g in range(pairs):
        for h in range(ring // 2):
            left = pieces_ref[g, lax.rem(2 * h - z + ring, ring)]
            right = pieces_ref[g, lax.rem(2 * h + 1 - z + ring, ring)]
            columns = slice((g * ring + 2 * h) * piece, (g * ring + 2 * h + 2) * piece)
            attention = lax.dot_general(
                key_ref[...],
                rope_ref[:, columns],
                (((0,), (0,)), ((), ())),
                preferred_element_type=jnp.float32,
            )
            routed = jnp.concatenate([left, right], axis=1)
            ready_ref[:, columns] = (routed + attention).astype(ready_ref.dtype)
            copy = pltpu.make_async_copy(
                ready_ref.at[:, columns], out_ref.at[:, columns], semaphores.at[len(copies)]
            )
            copy.start()
            copies.append(copy)
    for copy in copies:
        copy.wait()


def body(routes, route_weights, hidden_grads, expert_weight, normed, key_grad, rope_weight):
    groups = lax.axis_size(DP)
    experts_here = lax.axis_size(EXPERT)
    pairs = lax.axis_size("ylo")
    ring = lax.axis_size("z")
    slot_rows = hidden_grads[0]
    projection = expert_weight[0]
    depth = slot_rows.shape[1]
    capacity = slot_rows.shape[0] // experts_here
    piece = projection.shape[0]
    tokens, key_size = key_grad.shape
    key_lines = key_grad.T
    width = piece * groups
    share = width // experts_here
    last = ring // 2
    rows = experts_here * PAD
    z = lax.axis_index("z").astype(jnp.int32).reshape(1)
    low = (lax.axis_index("ylo") == 0).astype(jnp.int32).reshape(1)
    inner = [(i, (i + 1 - 2 * (i % 2)) % ring) for i in range(ring)]
    outer = [(i, (i - 1 + 2 * (i % 2)) % ring) for i in range(ring)]

    packed = key_size * share // 128
    cores = lax.axis_size("core")
    places = tuple(
        tuple(place * cores + core for core in range(cores)) for place in range(experts_here // cores)
    )
    swap = [(0, 1), (1, 0)]
    mine = call(
        functools.partial(partial_kernel, places),
        struct((len(places), packed, 128), jnp.float32),
        [SMEM] + [VMEM] * 4,
        4 * tokens * key_size * width,
        4 * 10**6,
    )(
        lax.axis_index("core").astype(jnp.int32).reshape(1),
        normed,
        key_lines,
        lax.ppermute(normed, "core", swap),
        lax.ppermute(key_lines, "core", swap),
    )
    terms = lax.all_to_all(mine, ("x", "yhi"), split_axis=0, concat_axis=0, tiled=True)

    other = lax.ppermute(slot_rows, "ylo", swap)

    def spaced_rows(other):
        return call(
            functools.partial(rows_kernel, capacity),
            struct((pairs, rows, depth), jnp.bfloat16),
            [SMEM, VMEM, VMEM],
            0,
            3 * 10**6,
        )(low, slot_rows, other).reshape(pairs * rows, depth)

    def products(weights, flops, after=()):
        columns = sum(w.shape[0] for w in weights)
        lines = -(-(-(-columns // 128) * capacity) // 16) * 16
        shape = (pairs * experts_here, lines, 128)
        return call(
            functools.partial(products_kernel, capacity),
            struct(shape, jnp.bfloat16),
            [VMEM] * (1 + len(weights)),
            flops,
            4 * 10**6,
            [pltpu.VMEM(shape, jnp.float32)],
            after,
        )(both, *weights)

    def added(sums, bit):
        return sums + lax.ppermute(sums, "z", [(i, i ^ bit) for i in range(ring)])

    def more_products(begun, columns, weights, flops, after=()):
        shape = (pairs * experts_here, 48, 128)
        return call(
            functools.partial(more_products_kernel, capacity, -(-columns // 128) * capacity),
            struct(shape, jnp.bfloat16),
            [VMEM] * (2 + len(weights)),
            flops,
            3 * 10**6,
            [pltpu.VMEM(shape, jnp.float32)],
            after,
        )(both, begun, *weights)

    def send(computed):
        return lax.all_to_all(computed, PLANE, split_axis=0, concat_axis=0, tiled=True)

    whole = -(-piece // 128) * 128
    layout = (
        ((0, 0), (whole, -1), (whole + piece, 1)),
        ((0, -2), (piece, 2)),
        ((0, -3), (piece, 3), (2 * piece, 4)),
    )
    paired, crossed = [projection], [projection]
    came = lax.ppermute(crossed[-1], "z", inner), lax.ppermute(paired[-1], "z", outer)
    paired.append(came[0])
    crossed.append(came[1])
    both = spaced_rows(other)
    begun = products([projection], 1 * 10**9)
    crossed[1], paired[1], begun = lax.optimization_barrier((crossed[1], paired[1], begun))
    first = more_products(begun, piece, [crossed[1], paired[1]], 2 * 10**9)
    first, terms = lax.optimization_barrier((first, terms))
    mine = jnp.sum(terms, axis=0)
    came = lax.ppermute(crossed[-1], "z", inner), lax.ppermute(paired[-1], "z", outer)
    paired.append(came[0])
    crossed.append(came[1])
    crossed[2], _ = lax.optimization_barrier((crossed[2], first))
    paired[2], _ = lax.optimization_barrier((paired[2], first))
    second = products([crossed[2], paired[2]], 15 * 10**9)
    came = lax.ppermute(crossed[-1], "z", inner), lax.ppermute(paired[-1], "z", outer)
    paired.append(came[0])
    crossed.append(came[1])
    sent = [send(first)]
    half = piece // 2

    def cut(array, start):
        return call(
            functools.partial(cut_kernel, start),
            struct((half, depth), jnp.bfloat16),
            [ANY],
            0,
            10**6,
            [pltpu.SemaphoreType.DMA],
            [second] + sent,
            ANY,
        )(array)

    half_low, half_high = cut(crossed[-1], 0), cut(paired[-1], half)
    last_low = lax.ppermute(half_low, "z", inner)
    last_high = lax.ppermute(half_high, "z", outer)
    sent.append(send(second))
    two = added(added(mine, 1), 2)
    begun = products([crossed[3], paired[3]], 10 * 10**9)
    third = more_products(begun, 2 * piece, [last_low, last_high], 1 * 10**9, [two])
    chunks = sent + [send(third)]

    combine = call(
        functools.partial(combine_kernel, experts_here, capacity),
        struct((tokens, rows), jnp.bfloat16),
        [VMEM, VMEM],
        10**7,
        10**6,
    )(routes, route_weights)
    most = max(chunk.shape[1] for chunk in chunks)
    lines = pltpu.VMEM((pairs * experts_here, most + PAD, 128), jnp.float32)
    summed = added(two, 4)
    summed = summed + lax.ppermute(summed, "ylo", swap)
    scale_factor = (tokens * groups * experts_here) ** (-0.5)
    rope_grad = call(
        functools.partial(rope_kernel, key_size, share, scale_factor),
        struct((key_size, share), jnp.float32),
        [VMEM],
        0,
        10**6,
    )(summed)

    token_grad = call(
        functools.partial(finish_kernel, capacity, layout),
        struct((tokens, width), jnp.bfloat16),
        [SMEM] + [VMEM] * (3 + len(chunks)),
        4 * 10**8,
        6 * 10**6,
        [
            pltpu.VMEM((pairs, ring, tokens, piece), jnp.float32),
            lines,
            pltpu.VMEM((tokens, width), jnp.bfloat16),
            pltpu.SemaphoreType.DMA((pairs * ring // 2,)),
        ],
        (),
        ANY,
    )(z, combine, key_lines, rope_weight, *chunks)
    return (token_grad, rope_grad)


def solution(mesh):
    wide = Mesh(mesh.devices.reshape(2, 8, 4, 4, 2), ALL)
    return jax.shard_map(
        body,
        mesh=wide,
        in_specs=(
            P(ALL, None),
            P(ALL, None),
            P(EXPERT, DP, None),
            P(EXPERT, DP, None),
            P(ALL, None),
            P(ALL, None),
            P(),
        ),
        out_specs=(P(ALL, None), P(None, EXPERT)),
        check_vma=False,
    )
```
